256 devices in a mesh: dp: 8 (over z_hi, y), segment: 32 (over z_lo, x, core).
Axes of the slice: x: 4, y: 4, z: 8 (z_hi: 2, z_lo: 4; z = z_hi * 4 + z_lo), core: 2. Of those that a mesh axis runs over, the one named last changes fastest.
Arguments:
- hidden_rows: float32 [4096, 2048], P('dp', 'segment'), may hold values from -10 to 10
- norm_gain: float32 [2048], replicated, may hold values from 0.25 to 1.75
- head_weight: bfloat16 [2048, 77824], P(None, 'segment'), may hold values from -1 to 1
- teacher_ids: int32 [4096, 32], P('dp'), may hold values from 0 to 77823, as said below
- teacher_logits: float32 [4096, 32], P('dp'), may hold values from -20 to 460
- token_weights: float32 [4096], P('dp'), may hold values from 0.5 to 10, as said below
Outputs:
- token_loss: float32 [4096], P('dp')
- mean_loss: float32 [], replicated
- grad_rows: float32 [4096, 2048], P('dp', 'segment')
The draws below stay inside these ranges and needn't reach their ends.
Inputs may be any that keep to these rules, and one draw needn't show every extreme that they name: `teacher_ids`: each row holds 32 different vocabulary indices. `token_weights`: positive.
All inputs are finite; a program needn't handle non-finite values.
Results may differ from the reference program's by a relative error of at most 0.0078.
Values may be sent and summed in bfloat16 or wider, within the bound.
A program may use at most 64 MiB of HBM per device.

```python
import math
import jax
import jax.numpy as jnp
from jax import lax

D = 2048
TOPK = 32
TOK_DEV = 512
VOCAB = 77824
TOKENS = 4096


def draw_hidden_rows(key, part):
    key = jax.random.fold_in(key, 11)
    subkeys = jax.random.split(key, 3)
    column_scale = 3.0 ** (jnp.arange(D, dtype=jnp.float32) / D)
    random_part = jnp.clip(jax.random.normal(subkeys[0], (TOKENS, D), jnp.float32), -6.0, 6.0)
    row_scale = jnp.exp(jax.random.uniform(subkeys[2], (TOKENS, 1), jnp.float32, math.log(0.05), math.log(0.5)))
    values = random_part * row_scale * column_scale[None, :]
    return values


def draw_head_weight(key, part):
    key = jax.random.fold_in(key, 12)
    spread = 6.0 / math.sqrt(D)
    values = jnp.clip(jax.random.normal(key, (D, VOCAB), jnp.float32), -6.0, 6.0) * spread
    return values.astype(jnp.bfloat16)


def draw_teacher_logits(key, part):
    key = jax.random.fold_in(key, 13)
    values = jnp.clip(jax.random.normal(key, (TOKENS, TOPK), jnp.float32) * 3.0, -18.0, 18.0)
    return values


def draw_teacher_ids(key, part):
    key = jax.random.fold_in(key, 17)
    subkeys = jax.random.split(key, 2)
    starts = jax.random.randint(subkeys[0], (TOKENS, 1), 0, VOCAB, jnp.int32)
    starts = starts.at[0, 0].set(VOCAB - 1).at[1, 0].set(0)
    spaces = jax.random.randint(subkeys[1], (TOKENS, TOPK), 1, VOCAB // TOPK + 1, jnp.int32)
    spaces = spaces.at[:, 0].set(0)
    return ((starts + jnp.cumsum(spaces, axis=1)) % VOCAB).astype(jnp.int32)


def draw_token_weights(key, part):
    key = jax.random.fold_in(key, 19)
    ramp_part = jnp.arange(TOKENS, dtype=jnp.float32) / TOKENS
    values = jnp.exp(jax.random.uniform(key, (TOKENS,), jnp.float32, math.log(0.5), math.log(2.0))) * (1.0 + 2.0 * ramp_part)
    return values


def setup_inputs(seed: int = 0) -> dict:
    key_list = jax.random.split(jax.random.key(seed), 7)
    hidden_rows = draw_hidden_rows(jax.random.fold_in(key_list[6], 71), 0)
    norm_gain = jnp.clip(1.0 + 0.15 * jax.random.normal(key_list[1], (D,), jnp.float32), 0.25, 1.75)
    head_weight = draw_head_weight(jax.random.fold_in(key_list[6], 71), 0)
    teacher_ids = draw_teacher_ids(jax.random.fold_in(key_list[6], 71), 0)
    teacher_logits = draw_teacher_logits(jax.random.fold_in(key_list[6], 71), 0)
    token_weights = draw_token_weights(jax.random.fold_in(key_list[6], 71), 0)
    return {"hidden_rows": hidden_rows, "norm_gain": norm_gain, "head_weight": head_weight, "teacher_ids": teacher_ids, "teacher_logits": teacher_logits, "token_weights": token_weights}


EPSILON = 1e-06

def reference(hidden_rows, norm_gain, head_weight, teacher_ids, teacher_logits, token_weights):
    weight_total = jnp.sum(token_weights)
    groups = TOKENS // TOK_DEV

    def block_terms(inputs):
        row_block, id_block, logit_block, weight_block = inputs
        squares = lax.optimization_barrier(jnp.sum(row_block * row_block, axis=1))
        inverse_rms = lax.rsqrt(squares / D + EPSILON)
        normed = (row_block * inverse_rms[:, None] * norm_gain[None, :]).astype(jnp.bfloat16)
        logits = jnp.dot(normed, head_weight, preferred_element_type=jnp.float32)
        row_max = lax.optimization_barrier(jnp.max(logits, axis=1))
        log_total = row_max + jnp.log(lax.optimization_barrier(jnp.sum(jnp.exp(logits - row_max[:, None]), axis=1)))
        teacher_max = lax.optimization_barrier(jnp.max(logit_block, axis=1, keepdims=True))
        shifted = logit_block - teacher_max
        teacher_logq = shifted - jnp.log(lax.optimization_barrier(jnp.sum(jnp.exp(shifted), axis=1, keepdims=True)))
        teacher_prob = jnp.exp(teacher_logq)
        picked = jnp.take_along_axis(logits, id_block, axis=1)
        token_loss = lax.optimization_barrier(jnp.sum(teacher_prob * teacher_logq, axis=1)) - lax.optimization_barrier(jnp.sum(teacher_prob * picked, axis=1)) + log_total
        coefficient = weight_block * TOKENS / weight_total
        row_index = jnp.arange(row_block.shape[0], dtype=jnp.int32)[:, None]
        targets = jnp.zeros_like(logits).at[row_index, id_block].add(teacher_prob)
        grad_logits = (coefficient[:, None] * (jnp.exp(logits - log_total[:, None]) - targets)).astype(jnp.bfloat16)
        grad_normed = lax.dot_general(grad_logits, head_weight, (((1,), (1,)), ((), ())), preferred_element_type=jnp.float32)
        scaled = grad_normed * norm_gain[None, :]
        dot_total = lax.optimization_barrier(jnp.sum(scaled * row_block, axis=1))
        grad_rows = inverse_rms[:, None] * (scaled - row_block * (inverse_rms * inverse_rms * dot_total / D)[:, None])
        return (token_loss, grad_rows)
    token_loss, grad_rows = lax.map(block_terms, (hidden_rows.reshape(groups, TOK_DEV, D), teacher_ids.reshape(groups, TOK_DEV, TOPK), teacher_logits.reshape(groups, TOK_DEV, TOPK), token_weights.reshape(groups, TOK_DEV)))
    token_loss = token_loss.reshape(TOKENS)
    mean_loss = jnp.sum(token_weights * token_loss) / weight_total
    return (token_loss, mean_loss, grad_rows.reshape(TOKENS, D))
```

```python
import functools

import jax
import jax.numpy as jnp
from jax import lax
from jax.experimental import pallas as pl
from jax.experimental.pallas import tpu as pltpu
from jax.sharding import PartitionSpec as P

D = 2048
EPSILON = 1e-06
NZ, NX, NC = 4, 4, 2
LOG2E = 1.4426950408889634
NT = (((1,), (1,)), ((), ()))
MESH = pl.DeviceIdType.MESH
F32, BF16 = jnp.float32, jnp.bfloat16


def kernel(
    cfg,
    h_hbm, g_hbm, w_hbm, ids_hbm, tl_hbm, wt_hbm,
    loss_out, mean_out, grad_out,
    h, g, w, ids, tl, wt,
    gcol, hb, lhs, logit, targ, gl, hi_x, lo_x, p1_x, p2_x,
    icol, acol, stat, sq1, sq2, st1, st2, dps, ent, rows,
    gs, sib_s, sib_r, rl_s, rl_r, dr_s, dr_r, z_s, z_r,
    lossv, meanv, gradv,
    local_sem, gath_r, gath_s, sq_r, sq_s, st_r, st_s, dp_r, dp_s, rs_r, rs_s,
):
    NB, TB, VS, ndp, tokens = cfg
    T = NB * TB
    Q = TB // 128
    FD = D // (NZ * NX * NC)
    VT = VS // 128
    seg = lax.axis_index("segment")
    dpi = lax.axis_index("dp")
    c = lax.rem(seg, NC)
    x = lax.rem(lax.div(seg, NC), NX)
    z = lax.div(seg, NC * NX)
    oc = 1 - c
    sends = []

    def at(zz, xx, cc):
        return (zz * NX + xx) * NC + cc

    sib = at(z, x, oc)
    xs = [x, lax.rem(x + 1, NX), lax.rem(x + 3, NX), lax.rem(x + 2, NX)]

    def zxor(d):
        if d == 1:
            return z + 1 - 2 * lax.rem(z, 2)
        if d == 2:
            return lax.rem(z + 2, 4)
        return 3 - z

    def remote(src, dst, ss, rs, seg_to):
        return pltpu.make_async_remote_copy(
            src_ref=src, dst_ref=dst, send_sem=ss, recv_sem=rs,
            device_id={"segment": seg_to}, device_id_type=MESH,
        )

    def send(src, dst, ss, rs, seg_to):
        cp = remote(src, dst, ss, rs, seg_to)
        cp.start()
        sends.append(cp)

    def wait_recv(dst, ss, rs):
        remote(dst, dst, ss, rs, sib).wait_recv()

    loads = [
        pltpu.make_async_copy(a, b, local_sem.at[i])
        for i, (a, b) in enumerate(
            [(h_hbm, h), (g_hbm, g), (tl_hbm, tl), (ids_hbm, ids), (wt_hbm, wt)]
        )
    ]
    for cp in loads:
        cp.start()
    wloads = [
        pltpu.make_async_copy(w_hbm.at[:, xs[i]], w.at[:, xs[i]], local_sem.at[5 + i])
        for i in range(NX)
    ]
    for cp in wloads:
        cp.start()
    barrier = pltpu.get_barrier_semaphore()
    partners = []
    for i in range(NX):
        for j in range(NC):
            if i or j:
                partners.append({"segment": at(z, xs[i], lax.rem(c + j, NC))})
    for d in (1, 2, 3):
        partners.append({"segment": at(zxor(d), x, c)})
    for d in range(1, ndp):
        partners.append({"dp": lax.rem(dpi + d, ndp)})
    for p in partners:
        pl.semaphore_signal(barrier, inc=1, device_id=p, device_id_type=MESH)

    loads[0].wait()
    loads[1].wait()
    grow = g[pl.ds(z * NX + x, 1), :]
    gcol[...] = jnp.transpose(jnp.broadcast_to(grow, (128, 128)))
    gown = gcol[pl.ds(c * FD, FD), :]
    hv = h[...]
    hg = hv * jnp.concatenate([gown] * (T // 128), axis=1)
    for b in range(NB):
        hb[b, z, x, c] = hg[:, b * TB : (b + 1) * TB].astype(BF16)
    sqrow = jnp.sum(hv * hv, axis=0, keepdims=True)
    slot = x * NC + c
    sq1[slot] = jnp.zeros((8, 128), F32)
    for r in range(T // 128):
        sq1[slot, r : r + 1, :] = sqrow[:, r * 128 : (r + 1) * 128]
    pl.semaphore_wait(barrier, len(partners))

    gath_count = [0] * NB

    def g_send(b, zz, xx, cc, seg_to):
        n = gath_count[b]
        gath_count[b] += 1
        ref = hb.at[b, zz, xx, cc]
        send(ref, ref, gath_s.at[b, n], gath_r.at[b, at(zz, xx, cc)], seg_to)

    def g_wait(b, zz, xx, cc):
        wait_recv(hb.at[b, zz, xx, cc], gath_s.at[b, 0], gath_r.at[b, at(zz, xx, cc)])

    def g_own(b):
        g_send(b, z, x, c, at(z, xs[1], c))
        g_send(b, z, x, c, at(z, xs[2], c))
        for d in (1, 2, 3):
            g_send(b, z, x, c, at(zxor(d), x, c))
        g_send(b, z, x, c, sib)

    def g_z(b):
        for d in (1, 2, 3):
            zz = zxor(d)
            g_wait(b, zz, x, c)
            g_send(b, zz, x, c, at(z, xs[1], c))
            g_send(b, zz, x, c, at(z, xs[2], c))
            g_send(b, zz, x, c, sib)

    def g_x(b):
        for d in (0, 1, 2, 3):
            zz = z if d == 0 else zxor(d)
            g_wait(b, zz, xs[2], c)
            g_wait(b, zz, xs[1], c)
            high = lax.div(zz, 2)
            src_x = xs[2] + high * (xs[1] - xs[2])
            dst_x = xs[1] + high * (xs[2] - xs[1])
            g_send(b, zz, src_x, c, at(z, dst_x, c))
            g_send(b, zz, xs[2], c, sib)
            g_send(b, zz, xs[1], c, sib)

    def g_relay(b):
        for d in (0, 1, 2, 3):
            zz = z if d == 0 else zxor(d)
            g_wait(b, zz, xs[3], c)
            g_send(b, zz, xs[3], c, sib)

    def l_col(b, i):
        xx = xs[i]
        for d in (0, 1, 2, 3):
            zz = z if d == 0 else zxor(d)
            g_wait(b, zz, xx, oc)
        if b == 0:
            wloads[i].wait()
        blk = hb[b, :, xx].reshape(NZ * NC * FD, TB)
        lhs[...] = jnp.transpose(blk)
        step = 768
        full = VS // step

        def tile(n0, width):
            wt_ = w[:, xx, :, pl.ds(n0, width)].reshape(NZ * NC * FD, width)
            r = jnp.dot(lhs[...], wt_, preferred_element_type=F32)
            if i == 0:
                logit[b, :, pl.ds(n0, width)] = r
            else:
                logit[b, :, pl.ds(n0, width)] += r

        def body(n, carry):
            tile(pl.multiple_of(n * step, 128), step)
            return carry

        if full:
            lax.fori_loop(0, full, body, 0)
        if VS - full * step:
            tile(full * step, VS - full * step)

    def sq_first():
        n = 0
        for i in range(NX):
            for j in range(NC):
                if i or j:
                    ref = sq1.at[slot]
                    send(ref, ref, sq_s.at[n], sq_r.at[slot], at(z, xs[i], lax.rem(c + j, NC)))
                    n += 1

    def sq_second():
        for i in range(NX):
            for j in range(NC):
                if i or j:
                    s_ = xs[i] * NC + lax.rem(c + j, NC)
                    wait_recv(sq1.at[s_], sq_s.at[0], sq_r.at[s_])
        sq2[z] = jnp.sum(sq1[...], axis=0)
        for d in (1, 2, 3):
            ref = sq2.at[z]
            send(ref, ref, sq_s.at[6 + d], sq_r.at[8 + z], at(zxor(d), x, c))

    def to_cols(v, r, ref, row0):
        col = jnp.transpose(jnp.broadcast_to(v[r : r + 1, :], (128, 128)))
        ref[pl.ds(row0, 128), :] = col

    def sq_final():
        for d in (1, 2, 3):
            s_ = zxor(d)
            wait_recv(sq2.at[s_], sq_s.at[0], sq_r.at[8 + s_])
        inv = lax.rsqrt(jnp.sum(sq2[...], axis=0) / D + EPSILON)
        rows[0] = inv
        for r in range(T // 128):
            to_cols(inv, r, icol, r * 128)

    def teacher():
        loads[2].wait()
        loads[3].wait()
        t = tl[...]
        sh = t - jnp.max(t, axis=0, keepdims=True)
        logq = sh - jnp.log(jnp.sum(jnp.exp(sh), axis=0, keepdims=True))
        p = jnp.exp(logq)
        hrow = jnp.sum(p * logq, axis=0, keepdims=True)
        for r in range(T // 128):
            ent[r : r + 1, :] = hrow[:, r * 128 : (r + 1) * 128]
        local = ids[...] - seg * VS
        valid = (local >= 0) & (local < VS)
        hi = jnp.where(valid, lax.shift_right_logical(jnp.where(valid, local, 0), 7), -1)
        lo = jnp.where(valid, local, 0) & 127
        p1 = p.astype(BF16).astype(F32)
        p2 = p - p1
        allv = jnp.concatenate([hi.astype(F32), lo.astype(F32), p1, p2], axis=0)
        k = p.shape[0]
        cols = jnp.transpose(allv).astype(BF16)
        lane = lax.broadcasted_iota(jnp.int32, (4 * k, 8 * k), 1)
        row = lax.broadcasted_iota(jnp.int32, (4 * k, 8 * k), 0)
        lk = lane & (k - 1)
        tok = lax.broadcasted_iota(jnp.int32, (T, 8 * k), 0) & 7
        tl_lane = lax.shift_right_logical(
            lax.broadcasted_iota(jnp.int32, (T, 8 * k), 1), 5
        )
        own = tok == tl_lane
        for j, ref in enumerate((hi_x, lo_x, p1_x, p2_x)):
            pick = jnp.where(row == lk + j * k, 1.0, 0.0).astype(BF16)
            v = jnp.dot(cols, pick, preferred_element_type=F32)
            ref[...] = v if j == 0 else jnp.where(own, v, 0.0)

    def targets(b, lo_blk, hi_blk):
        sub = lax.broadcasted_iota(jnp.int32, (128, 256), 0).astype(F32)

        def body(n, carry):
            r0 = pl.multiple_of(b * TB + n * 8, 8)
            hx = hi_x[pl.ds(r0, 8), :]
            a1 = p1_x[pl.ds(r0, 8), :]
            a2 = p2_x[pl.ds(r0, 8), :]
            lrow = jnp.sum(lo_x[pl.ds(r0, 8), :], axis=0, keepdims=True)
            bt = jnp.where(sub == lrow, 1.0, 0.0).astype(BF16)
            masks = [hx == float(j) for j in range(VT)]
            a = jnp.concatenate(
                [jnp.where(m, a1, 0.0) for m in masks]
                + [jnp.where(m, a2, 0.0) for m in masks],
                axis=0,
            ).astype(BF16)
            o = lax.dot_general(a, bt, NT, preferred_element_type=F32)
            o = o[: 8 * VT] + o[8 * VT :]
            for j in range(VT):
                targ[b, pl.ds(pl.multiple_of(n * 8, 8), 8), j * 128 : (j + 1) * 128] = (
                    o[j * 8 : (j + 1) * 8]
                )
            return carry

        lax.fori_loop(lo_blk, hi_blk, body, 0, unroll=2)

    def softmax(b):
        lane = lax.broadcasted_iota(jnp.int32, (8, 128), 1)

        def body(n, carry):
            r0 = pl.multiple_of(n * 8, 8)
            raw = [logit[b, pl.ds(r0, 8), j * 128 : (j + 1) * 128] for j in range(VT)]
            mx = functools.reduce(jnp.maximum, raw)
            mx = jnp.max(mx, axis=1, keepdims=True)
            iv = icol[pl.ds(pl.multiple_of(b * TB + n * 8, 8), 8), :]
            sc = iv * LOG2E
            m = jnp.broadcast_to(mx, (8, 128))
            s = jnp.zeros((8, 128), F32)
            sl = jnp.zeros((8, 128), F32)
            pk = jnp.zeros((8, 128), F32)
            for j in range(VT):
                e = jnp.exp2((raw[j] - m) * sc)
                logit[b, pl.ds(r0, 8), j * 128 : (j + 1) * 128] = e
                s += e
                sl += e * raw[j]
                pk += targ[b, pl.ds(r0, 8), j * 128 : (j + 1) * 128] * raw[j]
            s = jnp.sum(s, axis=1, keepdims=True)
            sl = jnp.sum(sl, axis=1, keepdims=True)
            pk = jnp.sum(pk, axis=1, keepdims=True)
            stat[pl.ds(r0, 8), :] = jnp.where(
                lane == 0, m * iv, jnp.where(lane == 1, s, jnp.where(lane == 2, sl, pk))
            )
            return carry

        lax.fori_loop(0, TB // 8, body, 0, unroll=2)
        for q in range(Q):
            tr = jnp.transpose(stat[q * 128 : (q + 1) * 128, :])
            for k in range(4):
                st1[b, slot, k * Q + q : k * Q + q + 1, :] = tr[k : k + 1, :]
        n = 0
        for i in range(NX):
            for j in range(NC):
                if i or j:
                    ref = st1.at[b, slot]
                    send(ref, ref, st_s.at[b, n], st_r.at[b, slot],
                         at(z, xs[i], lax.rem(c + j, NC)))
                    n += 1

    def merge(ref, b):
        m = ref[b, :, 0:Q, :]
        top = jnp.max(m, axis=0)
        wgt = jnp.exp(m - top[None])
        s = jnp.sum(wgt * ref[b, :, Q : 2 * Q, :], axis=0)
        sl = jnp.sum(wgt * ref[b, :, 2 * Q : 3 * Q, :], axis=0)
        pk = jnp.sum(ref[b, :, 3 * Q : 4 * Q, :], axis=0)
        return top, s, sl, pk

    def stat_second(b):
        for i in range(NX):
            for j in range(NC):
                if i or j:
                    s_ = xs[i] * NC + lax.rem(c + j, NC)
                    wait_recv(st1.at[b, s_], st_s.at[b, 0], st_r.at[b, s_])
        for k, v in enumerate(merge(st1, b)):
            st2[b, z, k * Q : (k + 1) * Q, :] = v
        for d in (1, 2, 3):
            ref = st2.at[b, z]
            send(ref, ref, st_s.at[b, 6 + d], st_r.at[b, 8 + z], at(zxor(d), x, c))

    def stat_final(b):
        for d in (1, 2, 3):
            s_ = zxor(d)
            wait_recv(st2.at[b, s_], st_s.at[b, 0], st_r.at[b, 8 + s_])
        top, s, sl, pk = merge(st2, b)
        total = top + jnp.log(s)
        inv = rows[0, b * Q : (b + 1) * Q, :]
        lossv[b * Q : (b + 1) * Q, :] = ent[b * Q : (b + 1) * Q, :] - inv * pk + total
        rows[1, b * Q : (b + 1) * Q, :] = sl / s - pk
        scale = jnp.exp(st1[b, slot, 0:Q, :] - total)
        for q in range(Q):
            to_cols(scale, q, acol, q * 128)

    def make_gl(b):
        def body(n, carry):
            r0 = pl.multiple_of(n * 16, 16)
            a = acol[pl.ds(r0, 16), :]
            for j in range(VT):
                sl_ = slice(j * 128, (j + 1) * 128)
                gl[pl.ds(r0, 16), sl_] = (
                    logit[b, pl.ds(r0, 16), sl_] * a - targ[b, pl.ds(r0, 16), sl_]
                ).astype(BF16)
            return carry

        lax.fori_loop(0, TB // 16, body, 0)

    order = [3, 1, 2, 0]

    def mm(b, k):
        xx = xs[order[k]]
        wt_ = w[:, xx].reshape(NZ * NC * FD, VS)
        r = lax.dot_general(wt_, gl[...], NT, preferred_element_type=F32)
        gs[k] = r.reshape(NZ, NC, FD, TB)
        sib_s[b, k] = gs[k, :, oc].astype(BF16)
        send(sib_s.at[b, k], sib_r.at[b, k], rs_s.at[b, k], rs_r.at[b, k], sib)

    def pair(b, k):
        wait_recv(sib_r.at[b, k], rs_s.at[b, 0], rs_r.at[b, k])
        return gs[k, :, c] + sib_r[b, k].astype(F32)

    def rs_col(b, k):
        v = pair(b, k)
        if k == 0:
            rl_s[b] = v.astype(BF16).reshape(2, 2, FD, TB)
            send(rl_s.at[b, 0], rl_r.at[b, 0], rs_s.at[b, 4], rs_r.at[b, 4], at(z, xs[1], c))
            send(rl_s.at[b, 1], rl_r.at[b, 1], rs_s.at[b, 5], rs_r.at[b, 5], at(z, xs[2], c))
        elif k in (1, 2):
            j = k - 1
            wait_recv(rl_r.at[b, j], rs_s.at[b, 0], rs_r.at[b, 4 + j])
            v = v.reshape(2, 2, FD, TB)
            dr_s[b, j, j] = (v[j] + rl_r[b, j].astype(F32)).astype(BF16)
            dr_s[b, j, 1 - j] = v[1 - j].astype(BF16)
            send(dr_s.at[b, j], dr_r.at[b, j], rs_s.at[b, 6 + j], rs_r.at[b, 6 + j],
                 at(z, xs[k], c))
        else:
            for j in (0, 1):
                wait_recv(dr_r.at[b, j], rs_s.at[b, 0], rs_r.at[b, 6 + j])
            v = v.reshape(2, 2, FD, TB) + dr_r[b, 0].astype(F32) + dr_r[b, 1].astype(F32)
            gs[3, :, 0] = v.reshape(NZ, FD, TB)
            z_s[b] = v.reshape(NZ, FD, TB).astype(BF16)
            for d in (1, 2, 3):
                zz = zxor(d)
                send(z_s.at[b, zz], z_r.at[b, z], rs_s.at[b, 7 + d], rs_r.at[b, 8 + z],
                     at(zz, x, c))
            gradv[:, b * TB : (b + 1) * TB] = gs[3, z, 0]

    def row_of(v, b):
        return jnp.concatenate([v[b * Q + q : b * Q + q + 1, :] for q in range(Q)], axis=1)

    def finish(b):
        cols = slice(b * TB, (b + 1) * TB)
        tot = gradv[:, cols]
        for d in (1, 2, 3):
            s_ = zxor(d)
            wait_recv(z_r.at[b, s_], rs_s.at[b, 0], rs_r.at[b, 8 + s_])
            tot = tot + z_r[b, s_].astype(F32)
        inv = rows[0]
        first = row_of(inv * rows[2], b)
        second = row_of(inv * inv * rows[1] / D, b)
        gn = jnp.concatenate([gcol[pl.ds(c * FD, FD), :]] * Q, axis=1)
        gradv[:, cols] = first * (gn * tot - h[:, cols] * second)

    def dp_send():
        wv = wt[...]
        lane_sum = lambda v: jnp.sum(jnp.sum(v, axis=1, keepdims=True), axis=0, keepdims=True)
        dps[dpi] = jnp.zeros((8, 128), F32)
        dps[dpi, 0:1, :] = jnp.broadcast_to(lane_sum(wv), (1, 128))
        dps[dpi, 1:2, :] = jnp.broadcast_to(lane_sum(wv * lossv[...]), (1, 128))
        for d in range(1, ndp):
            cp = pltpu.make_async_remote_copy(
                src_ref=dps.at[dpi], dst_ref=dps.at[dpi], send_sem=dp_s.at[d],
                recv_sem=dp_r.at[dpi], device_id={"dp": lax.rem(dpi + d, ndp)},
                device_id_type=MESH,
            )
            cp.start()
            sends.append(cp)

    def dp_final():
        for d in range(1, ndp):
            s_ = lax.rem(dpi + d, ndp)
            wait_recv(dps.at[s_], dp_s.at[0], dp_r.at[s_])
        tot = jnp.sum(dps[...], axis=0)
        meanv[...] = jnp.broadcast_to(tot[1:2, :] / tot[0:1, :], meanv.shape)
        rows[2, 0 : T // 128, :] = wt[...] * tokens / tot[0:1, :]

    nblk = TB // 8
    if NB == 1:
        g_own(0)
        sq_first()
        teacher()
        targets(0, 0, nblk // 4)
        g_z(0)
        sq_second()
        targets(0, nblk // 4, nblk // 2)
        l_col(0, 0)
        g_x(0)
        targets(0, nblk // 2, nblk)
        l_col(0, 1)
        g_relay(0)
        l_col(0, 2)
        sq_final()
        l_col(0, 3)
        softmax(0)
        loads[4].wait()
        stat_second(0)
        stat_final(0)
        dp_send()
        make_gl(0)
        mm(0, 0)
        mm(0, 1)
        rs_col(0, 0)
        mm(0, 2)
        rs_col(0, 1)
        mm(0, 3)
        rs_col(0, 2)
        dp_final()
        rs_col(0, 3)
        finish(0)
    else:
        g_own(0)
        sq_first()
        teacher()
        targets(0, 0, nblk // 2)
        g_z(0)
        g_own(1)
        sq_second()
        targets(0, nblk // 2, nblk)
        l_col(0, 0)
        g_x(0)
        g_z(1)
        l_col(0, 1)
        g_relay(0)
        l_col(0, 2)
        sq_final()
        g_x(1)
        l_col(0, 3)
        softmax(0)
        targets(1, 0, nblk)
        g_relay(1)
        l_col(1, 0)
        stat_second(0)
        l_col(1, 1)
        stat_final(0)
        make_gl(0)
        mm(0, 0)
        l_col(1, 2)
        rs_col(0, 0)
        l_col(1, 3)
        softmax(1)
        mm(0, 1)
        rs_col(0, 1)
        mm(0, 2)
        rs_col(0, 2)
        stat_second(1)
        mm(0, 3)
        stat_final(1)
        loads[4].wait()
        dp_send()
        rs_col(0, 3)
        make_gl(1)
        mm(1, 0)
        mm(1, 1)
        rs_col(1, 0)
        mm(1, 2)
        rs_col(1, 1)
        dp_final()
        finish(0)
        mm(1, 3)
        rs_col(1, 2)
        rs_col(1, 3)
        finish(1)

    outs = [
        pltpu.make_async_copy(a, b, local_sem.at[9 + i])
        for i, (a, b) in enumerate([(lossv, loss_out), (meanv, mean_out), (gradv, grad_out)])
    ]
    for cp in outs:
        cp.start()
    for cp in sends:
        cp.wait_send()
    for cp in outs:
        cp.wait()


NB_TOKENS = 2


def shards(hidden_rows, norm_gain, head_weight, teacher_ids, teacher_logits, token_weights):
    T, FD = hidden_rows.shape
    VS = head_weight.shape[1]
    K = teacher_ids.shape[1]
    ndp = lax.axis_size("dp")
    NB = NB_TOKENS
    TB = T // NB
    Q = TB // 128
    any_ = pl.BlockSpec(memory_space=pl.ANY)
    V = pltpu.VMEM
    dma = pltpu.SemaphoreType.DMA
    scratch = [
        V((FD, T), F32), V((NZ * NX, 128), F32), V((NZ, NX, NC * FD, VS), BF16),
        V((K, T), jnp.int32), V((K, T), F32), V((T // 128, 128), F32),
        V((128, 128), F32),
        V((NB, NZ, NX, NC, FD, TB), BF16),
        V((TB, NZ * NC * FD), BF16),
        V((NB, TB, VS), F32),
        V((NB, TB, VS), F32),
        V((TB, VS), BF16),
        V((T, 8 * K), F32), V((T, 8 * K), F32), V((T, 8 * K), F32), V((T, 8 * K), F32),
        V((T, 128), F32), V((TB, 128), F32), V((TB, 128), F32),
        V((NX * NC, 8, 128), F32), V((NZ, 8, 128), F32),
        V((NB, NX * NC, 4 * Q, 128), F32), V((NB, NZ, 4 * Q, 128), F32),
        V((ndp, 8, 128), F32), V((T // 128, 128), F32), V((3, 8, 128), F32),
        V((4, NZ, NC, FD, TB), F32),
        V((NB, 4, NZ, FD, TB), BF16), V((NB, 4, NZ, FD, TB), BF16),
        V((NB, 2, 2, FD, TB), BF16), V((NB, 2, 2, FD, TB), BF16),
        V((NB, 2, 2, 2, FD, TB), BF16), V((NB, 2, 2, 2, FD, TB), BF16),
        V((NB, NZ, FD, TB), BF16), V((NB, NZ, FD, TB), BF16),
        V((T // 128, 128), F32), V((8, 128), F32), V((FD, T), F32),
        dma((12,)), dma((NB, 32)), dma((NB, 31)), dma((12,)), dma((10,)),
        dma((NB, 12)), dma((NB, 10)), dma((ndp,)), dma((ndp,)), dma((NB, 12)), dma((NB, 11)),
    ]
    loss, mean, grad = pl.pallas_call(
        functools.partial(kernel, (NB, TB, VS, ndp, T * ndp)),
        out_shape=(
            jax.ShapeDtypeStruct((T // 128, 128), F32),
            jax.ShapeDtypeStruct((8, 128), F32),
            jax.ShapeDtypeStruct((FD, T), F32),
        ),
        in_specs=[any_] * 6,
        out_specs=(any_, any_, any_),
        scratch_shapes=scratch,
        compiler_params=pltpu.CompilerParams(
            collective_id=0, has_side_effects=True, vmem_limit_bytes=60 * 1024 * 1024
        ),
    )(
        hidden_rows.T,
        norm_gain.reshape(NZ * NX, 128),
        head_weight.reshape(NZ, NX, NC * FD, VS),
        teacher_ids.T,
        teacher_logits.T,
        token_weights.reshape(T // 128, 128),
    )
    return (loss.reshape(T), mean[0, 0], grad.T)


def solution(mesh):
    in_specs = (P("dp", "segment"), P(), P(None, "segment"), P("dp", None), P("dp", None), P("dp"))
    out_specs = (P("dp"), P(), P("dp", "segment"))
    return jax.shard_map(shards, mesh=mesh, in_specs=in_specs, out_specs=out_specs, check_vma=False)
```

```python
import functools

import jax
import jax.numpy as jnp
from jax import lax
from jax.experimental import pallas as pl
from jax.experimental.pallas import tpu as pltpu
from jax.sharding import PartitionSpec as P

D = 2048
EPSILON = 1e-06
NZ, NX, NC = 4, 4, 2
LOG2E = 1.4426950408889634
NT = (((1,), (1,)), ((), ()))
MESH = pl.DeviceIdType.MESH
F32, BF16 = jnp.float32, jnp.bfloat16


def kernel(
    cfg,
    h_hbm, g_hbm, w_hbm, ids_hbm, tl_hbm, wt_hbm,
    loss_out, mean_out, grad_out,
    h, g, w, ids, tl, wt,
    gcol, hb, lhs, logit, targ, gl, hi_x, lo_x, p1_x, p2_x,
    icol, acol, stat, sq1, sq2, st1, st2, dps, ent, rows,
    gs, sib_s, sib_r, rl_s, rl_r, dr_s, dr_r, z_s, z_r,
    lossv, meanv, gradv,
    local_sem, gath_r, gath_s, sq_r, sq_s, st_r, st_s, dp_r, dp_s, rs_r, rs_s,
):
    NB, TB, VS, ndp, tokens = cfg
    T = NB * TB
    Q = TB // 128
    FD = D // (NZ * NX * NC)
    VT = VS // 128
    seg = lax.axis_index("segment")
    dpi = lax.axis_index("dp")
    c = lax.rem(seg, NC)
    x = lax.rem(lax.div(seg, NC), NX)
    z = lax.div(seg, NC * NX)
    oc = 1 - c
    sends = []

    def at(zz, xx, cc):
        return (zz * NX + xx) * NC + cc

    sib = at(z, x, oc)
    xs = [x, lax.rem(x + 1, NX), lax.rem(x + 3, NX), lax.rem(x + 2, NX)]

    def zxor(d):
        if d == 1:
            return z + 1 - 2 * lax.rem(z, 2)
        if d == 2:
            return lax.rem(z + 2, 4)
        return 3 - z

    def remote(src, dst, ss, rs, seg_to):
        return pltpu.make_async_remote_copy(
            src_ref=src, dst_ref=dst, send_sem=ss, recv_sem=rs,
            device_id={"segment": seg_to}, device_id_type=MESH,
        )

    def send(src, dst, ss, rs, seg_to):
        cp = remote(src, dst, ss, rs, seg_to)
        cp.start()
        sends.append(cp)

    def wait_recv(dst, ss, rs):
        remote(dst, dst, ss, rs, sib).wait_recv()

    loads = [
        pltpu.make_async_copy(a, b, local_sem.at[i])
        for i, (a, b) in enumerate(
            [(h_hbm, h), (g_hbm, g), (tl_hbm, tl), (ids_hbm, ids), (wt_hbm, wt)]
        )
    ]
    for cp in loads:
        cp.start()
    wloads = [
        pltpu.make_async_copy(w_hbm.at[:, xs[i]], w.at[:, xs[i]], local_sem.at[5 + i])
        for i in range(NX)
    ]
    for cp in wloads:
        cp.start()
    barrier = pltpu.get_barrier_semaphore()
    partners = []
    for i in range(NX):
        for j in range(NC):
            if i or j:
                partners.append({"segment": at(z, xs[i], lax.rem(c + j, NC))})
    for d in (1, 2, 3):
        partners.append({"segment": at(zxor(d), x, c)})
    for d in range(1, ndp):
        partners.append({"dp": lax.rem(dpi + d, ndp)})
    for p in partners:
        pl.semaphore_signal(barrier, inc=1, device_id=p, device_id_type=MESH)

    loads[0].wait()
    loads[1].wait()
    grow = g[pl.ds(z * NX + x, 1), :]
    gcol[...] = jnp.transpose(jnp.broadcast_to(grow, (128, 128)))
    gown = gcol[pl.ds(c * FD, FD), :]
    hv = h[...]
    hg = hv * jnp.concatenate([gown] * (T // 128), axis=1)
    for b in range(NB):
        hb[b, z, x, c] = hg[:, b * TB : (b + 1) * TB].astype(BF16)
    sqrow = jnp.sum(hv * hv, axis=0, keepdims=True)
    slot = x * NC + c
    sq1[slot] = jnp.zeros((8, 128), F32)
    for r in range(T // 128):
        sq1[slot, r : r + 1, :] = sqrow[:, r * 128 : (r + 1) * 128]
    pl.semaphore_wait(barrier, len(partners))

    gath_count = [0] * NB

    def g_send(b, zz, xx, cc, seg_to):
        n = gath_count[b]
        gath_count[b] += 1
        ref = hb.at[b, zz, xx, cc]
        send(ref, ref, gath_s.at[b, n], gath_r.at[b, at(zz, xx, cc)], seg_to)

    def g_wait(b, zz, xx, cc):
        wait_recv(hb.at[b, zz, xx, cc], gath_s.at[b, 0], gath_r.at[b, at(zz, xx, cc)])

    def g_own(b):
        g_send(b, z, x, c, at(z, xs[1], c))
        g_send(b, z, x, c, at(z, xs[2], c))
        for d in (1, 3, 2):
            g_send(b, z, x, c, at(zxor(d), x, c))
        g_send(b, z, x, c, sib)

    def g_z(b, steps=(1, 3, 2)):
        for d in steps:
            zz = zxor(d)
            g_wait(b, zz, x, c)
            g_send(b, zz, x, c, at(z, xs[1], c))
            g_send(b, zz, x, c, at(z, xs[2], c))
            g_send(b, zz, x, c, sib)

    HR = FD // 2

    def g_half(b, zz, xx, j):
        return hb.at[b, zz, xx, c, pl.ds(j * HR, HR)]

    def g_half_sem(b, zz, xx, j):
        return gath_r.at[b, at(zz, xx, c) if j == 0 else 32 + zz]

    def g_x(b):
        for d in (0, 1, 3, 2):
            zz = z if d == 0 else zxor(d)
            for j, (src, dst) in enumerate(((xs[2], xs[1]), (xs[1], xs[2]))):
                g_wait(b, zz, src, c)
                n = gath_count[b]
                gath_count[b] += 1
                ref = g_half(b, zz, src, j)
                send(ref, ref, gath_s.at[b, n], g_half_sem(b, zz, src, j), at(z, dst, c))
                g_send(b, zz, src, c, sib)

    def g_relay(b):
        for d in (0, 1, 3, 2):
            zz = z if d == 0 else zxor(d)
            for j in (0, 1):
                wait_recv(g_half(b, zz, xs[3], j), gath_s.at[b, 0], g_half_sem(b, zz, xs[3], j))
            g_send(b, zz, xs[3], c, sib)

    def l_col(b, i):
        xx = xs[i]
        for d in (0, 1, 2, 3):
            zz = z if d == 0 else zxor(d)
            g_wait(b, zz, xx, oc)
        if b == 0:
            wloads[i].wait()
        blk = hb[b, :, xx].reshape(NZ * NC * FD, TB)
        lhs[...] = jnp.transpose(blk)
        wt_ = w[:, xx].reshape(NZ * NC * FD, VS)
        r = jnp.dot(lhs[...], wt_, preferred_element_type=F32)
        if i == 0:
            logit[b] = r
            return
        r = r + logit[b]
        logit[b] = r
        if i == NX - 1:
            tops = [r[:, j * 128 : (j + 1) * 128] for j in range(VT)]
            stat[3] = functools.reduce(jnp.maximum, tops)

    def sq_first():
        n = 0
        for i in range(NX):
            for j in range(NC):
                if i or j:
                    ref = sq1.at[slot]
                    send(ref, ref, sq_s.at[n], sq_r.at[slot], at(z, xs[i], lax.rem(c + j, NC)))
                    n += 1

    def sq_second():
        for i in range(NX):
            for j in range(NC):
                if i or j:
                    s_ = xs[i] * NC + lax.rem(c + j, NC)
                    wait_recv(sq1.at[s_], sq_s.at[0], sq_r.at[s_])
        sq2[z] = jnp.sum(sq1[...], axis=0)
        for d in (1, 2, 3):
            ref = sq2.at[z]
            send(ref, ref, sq_s.at[6 + d], sq_r.at[8 + z], at(zxor(d), x, c))

    def to_cols(v, r, ref, row0):
        col = jnp.transpose(jnp.broadcast_to(v[r : r + 1, :], (128, 128)))
        ref[pl.ds(row0, 128), :] = col

    def sq_final():
        for d in (1, 2, 3):
            s_ = zxor(d)
            wait_recv(sq2.at[s_], sq_s.at[0], sq_r.at[8 + s_])
        inv = lax.rsqrt(jnp.sum(sq2[...], axis=0) / D + EPSILON)
        rows[0] = inv
        for r in range(T // 128):
            to_cols(inv, r, icol, r * 128)

    def teacher():
        loads[2].wait()
        loads[3].wait()
        t = tl[...]
        sh = t - jnp.max(t, axis=0, keepdims=True)
        logq = sh - jnp.log(jnp.sum(jnp.exp(sh), axis=0, keepdims=True))
        p = jnp.exp(logq)
        hrow = jnp.sum(p * logq, axis=0, keepdims=True)
        for r in range(T // 128):
            ent[r : r + 1, :] = hrow[:, r * 128 : (r + 1) * 128]
        local = ids[...] - seg * VS
        valid = (local >= 0) & (local < VS)
        hi = jnp.where(valid, lax.shift_right_logical(jnp.where(valid, local, 0), 7), -1)
        lo = jnp.where(valid, local, 0) & 127
        p1 = p.astype(BF16).astype(F32)
        p2 = p - p1
        allv = jnp.concatenate([hi.astype(F32), lo.astype(F32), p1, p2], axis=0)
        k = p.shape[0]
        cols = jnp.transpose(allv).astype(BF16)
        lane = lax.broadcasted_iota(jnp.int32, (4 * k, 8 * k), 1)
        row = lax.broadcasted_iota(jnp.int32, (4 * k, 8 * k), 0)
        lk = lane & (k - 1)
        tok = lax.broadcasted_iota(jnp.int32, (T, 8 * k), 0) & 7
        tl_lane = lax.shift_right_logical(
            lax.broadcasted_iota(jnp.int32, (T, 8 * k), 1), 5
        )
        own = tok == tl_lane
        for j, ref in enumerate((hi_x, lo_x, p1_x, p2_x)):
            pick = jnp.where(row == lk + j * k, 1.0, 0.0).astype(BF16)
            v = jnp.dot(cols, pick, preferred_element_type=F32)
            ref[...] = v if j == 0 else jnp.where(own, v, 0.0)

    def targets(b, lo_blk, hi_blk):
        sub = lax.broadcasted_iota(jnp.int32, (128, 256), 0).astype(F32).astype(BF16)
        half = (lax.broadcasted_iota(jnp.int32, (16, 256), 0) // 8).astype(F32).astype(BF16)
        nh = (VT + 1) // 2
        one, zero = jnp.ones((), BF16), jnp.zeros((), BF16)

        def twice(v):
            return jnp.concatenate([v, v], axis=0).astype(BF16)

        def body(n, carry):
            r0 = pl.multiple_of(b * TB + n * 8, 8)
            hx = twice(hi_x[pl.ds(r0, 8), :]) - half
            a1 = twice(p1_x[pl.ds(r0, 8), :])
            a2 = twice(p2_x[pl.ds(r0, 8), :])
            lrow = jnp.sum(lo_x[pl.ds(r0, 8), :], axis=0, keepdims=True).astype(BF16)
            bt = jnp.where(sub == lrow, one, zero)
            masks = [hx == jnp.asarray(2.0 * j, BF16) for j in range(nh)]
            a = jnp.concatenate(
                [jnp.where(m, a1, zero) for m in masks]
                + [jnp.where(m, a2, zero) for m in masks],
                axis=0,
            )
            o = lax.dot_general(a, bt, NT, preferred_element_type=F32)
            o = o[: 16 * nh] + o[16 * nh :]
            for j in range(VT):
                targ[b, pl.ds(pl.multiple_of(n * 8, 8), 8), j * 128 : (j + 1) * 128] = (
                    o[j * 8 : (j + 1) * 8]
                )
            return carry

        lax.fori_loop(lo_blk, hi_blk, body, 0, unroll=4)

    def softmax(b):
        R = 32
        tops = stat[3]
        for q in range(Q):
            tr = jnp.transpose(tops[q * 128 : (q + 1) * 128])
            mrow = jnp.max(tr, axis=0, keepdims=True)
            r = b * Q + q
            st1[b, slot, q : q + 1, :] = mrow * rows[0, r : r + 1, :]
        stat[3] = jnp.broadcast_to(jnp.max(tops, axis=1, keepdims=True), (TB, 128))

        def body(n, carry):
            r0 = pl.multiple_of(n * R, R)
            sc = icol[pl.ds(pl.multiple_of(b * TB + n * R, R), R), :] * LOG2E
            m = stat[3, pl.ds(r0, R), :]
            s = jnp.zeros((R, 128), F32)
            sl = jnp.zeros((R, 128), F32)
            pk = jnp.zeros((R, 128), F32)
            for j in range(VT):
                raw = logit[b, pl.ds(r0, R), j * 128 : (j + 1) * 128]
                e = jnp.exp2((raw - m) * sc)
                logit[b, pl.ds(r0, R), j * 128 : (j + 1) * 128] = e
                s += e
                sl += e * raw
                pk += targ[b, pl.ds(r0, R), j * 128 : (j + 1) * 128] * raw
            stat[0, pl.ds(r0, R), :] = s
            stat[1, pl.ds(r0, R), :] = sl
            stat[2, pl.ds(r0, R), :] = pk
            return carry

        lax.fori_loop(0, TB // R, body, 0, unroll=2)
        for q in range(Q):
            for k in range(3):
                tr = jnp.transpose(stat[k, q * 128 : (q + 1) * 128, :])
                r = (k + 1) * Q + q
                st1[b, slot, r : r + 1, :] = jnp.sum(tr, axis=0, keepdims=True)
        n = 0
        for i in range(NX):
            for j in range(NC):
                if i or j:
                    ref = st1.at[b, slot]
                    send(ref, ref, st_s.at[b, n], st_r.at[b, slot],
                         at(z, xs[i], lax.rem(c + j, NC)))
                    n += 1

    def merge(ref, b):
        m = ref[b, :, 0:Q, :]
        top = jnp.max(m, axis=0)
        wgt = jnp.exp(m - top[None])
        s = jnp.sum(wgt * ref[b, :, Q : 2 * Q, :], axis=0)
        sl = jnp.sum(wgt * ref[b, :, 2 * Q : 3 * Q, :], axis=0)
        pk = jnp.sum(ref[b, :, 3 * Q : 4 * Q, :], axis=0)
        return top, s, sl, pk

    def stat_second(b):
        for i in range(NX):
            for j in range(NC):
                if i or j:
                    s_ = xs[i] * NC + lax.rem(c + j, NC)
                    wait_recv(st1.at[b, s_], st_s.at[b, 0], st_r.at[b, s_])
        for k, v in enumerate(merge(st1, b)):
            st2[b, z, k * Q : (k + 1) * Q, :] = v
        for d in (1, 2, 3):
            ref = st2.at[b, z]
            send(ref, ref, st_s.at[b, 6 + d], st_r.at[b, 8 + z], at(zxor(d), x, c))

    def stat_final(b):
        for d in (1, 2, 3):
            s_ = zxor(d)
            wait_recv(st2.at[b, s_], st_s.at[b, 0], st_r.at[b, 8 + s_])
        top, s, sl, pk = merge(st2, b)
        total = top + jnp.log(s)
        inv = rows[0, b * Q : (b + 1) * Q, :]
        lossv[b * Q : (b + 1) * Q, :] = ent[b * Q : (b + 1) * Q, :] - inv * pk + total
        rows[1, b * Q : (b + 1) * Q, :] = sl / s - pk
        scale = jnp.exp(st1[b, slot, 0:Q, :] - total)
        for q in range(Q):
            to_cols(scale, q, acol, q * 128)

    def make_gl(b):
        def body(n, carry):
            r0 = pl.multiple_of(n * 16, 16)
            a = acol[pl.ds(r0, 16), :]
            for j in range(VT):
                sl_ = slice(j * 128, (j + 1) * 128)
                gl[pl.ds(r0, 16), sl_] = (
                    logit[b, pl.ds(r0, 16), sl_] * a - targ[b, pl.ds(r0, 16), sl_]
                ).astype(BF16)
            return carry

        lax.fori_loop(0, TB // 16, body, 0)

    order = [3, 1, 2, 0]

    def mm(b, k):
        xx = xs[order[k]]
        wt_ = w[:, xx].reshape(NZ * NC * FD, VS)
        r = lax.dot_general(wt_, gl[...], NT, preferred_element_type=F32)
        gs[b, k] = r.reshape(NZ, NC, FD, TB)
        sib_s[b, k] = gs[b, k, :, oc].astype(BF16)
        send(sib_s.at[b, k], sib_r.at[b, k], rs_s.at[b, k], rs_r.at[b, k], sib)

    def pair(b, k):
        wait_recv(sib_r.at[b, k], rs_s.at[b, 0], rs_r.at[b, k])
        return gs[b, k, :, c] + sib_r[b, k].astype(F32)

    def rs_col(b, k):
        v = pair(b, k)
        if k == 0:
            for j in (0, 1):
                rl_s[b, j] = v[:, j * HR : (j + 1) * HR].astype(BF16)
            for d in (1, 3, 2, 0):
                zz = z if d == 0 else zxor(d)
                for j in (0, 1):
                    n = 4 + 4 * j + zz
                    send(rl_s.at[b, j, zz], rl_r.at[b, j, zz], rs_s.at[b, n], rs_r.at[b, n],
                         at(z, xs[1 + j], c))
            return
        gs[b, k, :, 0] = v
        if k in (1, 2):
            j = k - 1
            for d in (1, 3, 2, 0):
                zz = z if d == 0 else zxor(d)
                wait_recv(rl_r.at[b, j, zz], rs_s.at[b, 0], rs_r.at[b, 4 + 4 * j + zz])
                u = gs[b, k, zz, 0]
                part = u[j * HR : (j + 1) * HR] + rl_r[b, j, zz].astype(F32)
                rest = u[(1 - j) * HR : (2 - j) * HR]
                dr_s[b, j, zz] = jnp.concatenate(
                    [part, rest] if j == 0 else [rest, part], axis=0
                ).astype(BF16)
                n = 12 + 4 * j + zz
                send(dr_s.at[b, j, zz], dr_r.at[b, j, zz], rs_s.at[b, n], rs_r.at[b, n],
                     at(z, xs[k], c))
            return
        for d in (1, 3, 2, 0):
            zz = z if d == 0 else zxor(d)
            for j in (0, 1):
                wait_recv(dr_r.at[b, j, zz], rs_s.at[b, 0], rs_r.at[b, 12 + 4 * j + zz])
            u = gs[b, 3, zz, 0] + dr_r[b, 0, zz].astype(F32) + dr_r[b, 1, zz].astype(F32)
            if d:
                z_s[b, zz] = u.astype(BF16)
                send(z_s.at[b, zz], z_r.at[b, z], rs_s.at[b, 19 + d], rs_r.at[b, 20 + z],
                     at(zz, x, c))
            else:
                gradv[:, b * TB : (b + 1) * TB] = u

    def row_of(v, b):
        return jnp.concatenate([v[b * Q + q : b * Q + q + 1, :] for q in range(Q)], axis=1)

    def finish(b):
        cols = slice(b * TB, (b + 1) * TB)
        tot = gradv[:, cols]
        for d in (1, 2, 3):
            s_ = zxor(d)
            wait_recv(z_r.at[b, s_], rs_s.at[b, 0], rs_r.at[b, 20 + s_])
            tot = tot + z_r[b, s_].astype(F32)
        inv = rows[0]
        first = row_of(inv * rows[2], b)
        second = row_of(inv * inv * rows[1] / D, b)
        gn = jnp.concatenate([gcol[pl.ds(c * FD, FD), :]] * Q, axis=1)
        gradv[:, cols] = first * (gn * tot - h[:, cols] * second)

    def dp_send():
        wv = wt[...]
        lane_sum = lambda v: jnp.sum(jnp.sum(v, axis=1, keepdims=True), axis=0, keepdims=True)
        dps[dpi] = jnp.zeros((8, 128), F32)
        dps[dpi, 0:1, :] = jnp.broadcast_to(lane_sum(wv), (1, 128))
        dps[dpi, 1:2, :] = jnp.broadcast_to(lane_sum(wv * lossv[...]), (1, 128))
        for d in range(1, ndp):
            cp = pltpu.make_async_remote_copy(
                src_ref=dps.at[dpi], dst_ref=dps.at[dpi], send_sem=dp_s.at[d],
                recv_sem=dp_r.at[dpi], device_id={"dp": lax.rem(dpi + d, ndp)},
                device_id_type=MESH,
            )
            cp.start()
            sends.append(cp)

    def dp_final():
        for d in range(1, ndp):
            s_ = lax.rem(dpi + d, ndp)
            wait_recv(dps.at[s_], dp_s.at[0], dp_r.at[s_])
        tot = jnp.sum(dps[...], axis=0)
        meanv[...] = jnp.broadcast_to(tot[1:2, :] / tot[0:1, :], meanv.shape)
        rows[2, 0 : T // 128, :] = wt[...] * tokens / tot[0:1, :]

    nblk = TB // 8
    if NB == 1:
        g_own(0)
        sq_first()
        teacher()
        targets(0, 0, nblk // 4)
        g_z(0)
        sq_second()
        targets(0, nblk // 4, nblk // 2)
        l_col(0, 0)
        g_x(0)
        targets(0, nblk // 2, nblk)
        l_col(0, 1)
        g_relay(0)
        l_col(0, 2)
        sq_final()
        l_col(0, 3)
        softmax(0)
        loads[4].wait()
        stat_second(0)
        stat_final(0)
        dp_send()
        make_gl(0)
        mm(0, 0)
        mm(0, 1)
        rs_col(0, 0)
        mm(0, 2)
        rs_col(0, 1)
        mm(0, 3)
        rs_col(0, 2)
        dp_final()
        rs_col(0, 3)
        finish(0)
    else:
        g_own(0)
        sq_first()
        g_own(1)
        teacher()
        targets(0, 0, nblk // 4)
        g_z(0, (1,))
        targets(0, nblk // 4, nblk)
        g_z(0, (3, 2))
        sq_second()
        targets(1, 0, nblk // 2)
        g_x(0)
        l_col(0, 0)
        g_z(1)
        targets(1, nblk // 2, nblk)
        g_relay(0)
        l_col(0, 1)
        l_col(0, 2)
        g_x(1)
        sq_final()
        l_col(0, 3)
        softmax(0)
        l_col(1, 0)
        g_relay(1)
        l_col(1, 1)
        l_col(1, 2)
        stat_second(0)
        l_col(1, 3)
        softmax(1)
        stat_final(0)
        make_gl(0)
        mm(0, 0)
        mm(0, 1)
        rs_col(0, 0)
        stat_second(1)
        mm(0, 2)
        mm(0, 3)
        rs_col(0, 1)
        rs_col(0, 2)
        stat_final(1)
        make_gl(1)
        loads[4].wait()
        mm(1, 0)
        mm(1, 1)
        rs_col(1, 0)
        dp_send()
        mm(1, 2)
        mm(1, 3)
        rs_col(1, 1)
        rs_col(1, 2)
        rs_col(0, 3)
        dp_final()
        finish(0)
        rs_col(1, 3)
        finish(1)

    outs = [
        pltpu.make_async_copy(a, b, local_sem.at[9 + i])
        for i, (a, b) in enumerate([(lossv, loss_out), (meanv, mean_out), (gradv, grad_out)])
    ]
    for cp in outs:
        cp.start()
    for cp in sends:
        cp.wait_send()
    for cp in outs:
        cp.wait()


NB_TOKENS = 2


def write_out(loss, mean, grad, loss_out, mean_out, grad_out):
    loss_out[...] = loss[...]
    mean_out[...] = mean[0:1, 0:1]
    grad_out[...] = grad[...]


def shards(hidden_rows, norm_gain, head_weight, teacher_ids, teacher_logits, token_weights):
    T, FD = hidden_rows.shape
    VS = head_weight.shape[1]
    K = teacher_ids.shape[1]
    ndp = lax.axis_size("dp")
    NB = NB_TOKENS
    TB = T // NB
    Q = TB // 128
    any_ = pl.BlockSpec(memory_space=pl.ANY)
    V = pltpu.VMEM
    dma = pltpu.SemaphoreType.DMA
    scratch = [
        V((FD, T), F32), V((NZ * NX, 128), F32), V((NZ, NX, NC * FD, VS), BF16),
        V((K, T), jnp.int32), V((K, T), F32), V((T // 128, 128), F32),
        V((128, 128), F32),
        V((NB, NZ, NX, NC, FD, TB), BF16),
        V((TB, NZ * NC * FD), BF16),
        V((NB, TB, VS), F32),
        V((NB, TB, VS), F32),
        V((TB, VS), BF16),
        V((T, 8 * K), F32), V((T, 8 * K), F32), V((T, 8 * K), F32), V((T, 8 * K), F32),
        V((T, 128), F32), V((TB, 128), F32), V((4, TB, 128), F32),
        V((NX * NC, 8, 128), F32), V((NZ, 8, 128), F32),
        V((NB, NX * NC, 4 * Q, 128), F32), V((NB, NZ, 4 * Q, 128), F32),
        V((ndp, 8, 128), F32), V((T // 128, 128), F32), V((3, 8, 128), F32),
        V((NB, 4, NZ, NC, FD, TB), F32),
        V((NB, 4, NZ, FD, TB), BF16), V((NB, 4, NZ, FD, TB), BF16),
        V((NB, 2, NZ, FD // 2, TB), BF16), V((NB, 2, NZ, FD // 2, TB), BF16),
        V((NB, 2, NZ, FD, TB), BF16), V((NB, 2, NZ, FD, TB), BF16),
        V((NB, NZ, FD, TB), BF16), V((NB, NZ, FD, TB), BF16),
        V((T // 128, 128), F32), V((8, 128), F32), V((FD, T), F32),
        dma((12,)), dma((NB, 36)), dma((NB, 35)), dma((12,)), dma((10,)),
        dma((NB, 12)), dma((NB, 10)), dma((ndp,)), dma((ndp,)), dma((NB, 24)), dma((NB, 23)),
    ]
    loss, mean, grad = pl.pallas_call(
        functools.partial(kernel, (NB, TB, VS, ndp, T * ndp)),
        out_shape=(
            jax.ShapeDtypeStruct((T // 128, 128), F32),
            jax.ShapeDtypeStruct((8, 128), F32),
            jax.ShapeDtypeStruct((FD, T), F32),
        ),
        in_specs=[any_] * 6,
        out_specs=(any_, any_, any_),
        scratch_shapes=scratch,
        compiler_params=pltpu.CompilerParams(
            collective_id=0, has_side_effects=True, vmem_limit_bytes=60 * 1024 * 1024
        ),
    )(
        hidden_rows.T,
        norm_gain.reshape(NZ * NX, 128),
        head_weight.reshape(NZ, NX, NC * FD, VS),
        teacher_ids.T,
        teacher_logits.T,
        token_weights.reshape(T // 128, 128),
    )
    loss, mean, grad = pl.pallas_call(
        write_out,
        out_shape=(
            jax.ShapeDtypeStruct((T // 128, 128), F32),
            jax.ShapeDtypeStruct((1, 1), F32),
            jax.ShapeDtypeStruct((FD, T), F32),
        ),
    )(loss, mean, grad)
    return (loss.reshape(T), mean.reshape(()), grad.T)


def solution(mesh):
    in_specs = (P("dp", "segment"), P(), P(None, "segment"), P("dp", None), P("dp", None), P("dp"))
    out_specs = (P("dp"), P(), P("dp", "segment"))
    return jax.shard_map(shards, mesh=mesh, in_specs=in_specs, out_specs=out_specs, check_vma=False)
```

```python
import functools

import jax
import jax.numpy as jnp
from jax import lax
from jax.experimental import pallas as pl
from jax.experimental.pallas import tpu as pltpu
from jax.sharding import PartitionSpec as P

D = 2048
EPSILON = 1e-06
NZ, NX, NC = 4, 4, 2
LOG2E = 1.4426950408889634
NT = (((1,), (1,)), ((), ()))
MESH = pl.DeviceIdType.MESH
F32, BF16 = jnp.float32, jnp.bfloat16


def kernel(
    cfg,
    h_hbm, g_hbm, w_hbm, ids_hbm, tl_hbm, wt_hbm,
    loss_out, mean_out, grad_out,
    h, g, w, ids, tl, wt,
    gcol, hb, lhs, logit, targ, gl, hi_x, lo_x, p1_x, p2_x,
    icol, acol, stat, sq1, sq2, st1, st2, dps, ent, rows,
    gs, sib_s, sib_r, rl_s, rl_r, dr_s, dr_r, z_s, z_r,
    lossv, meanv, gradv,
    local_sem, gath_r, gath_s, sq_r, sq_s, st_r, st_s, dp_r, dp_s, rs_r, rs_s,
):
    NB, TB, VS, ndp, tokens = cfg
    T = NB * TB
    Q = TB // 128
    FD = D // (NZ * NX * NC)
    VT = VS // 128
    seg = lax.axis_index("segment")
    dpi = lax.axis_index("dp")
    c = lax.rem(seg, NC)
    x = lax.rem(lax.div(seg, NC), NX)
    z = lax.div(seg, NC * NX)
    oc = 1 - c
    sends = []

    def at(zz, xx, cc):
        return (zz * NX + xx) * NC + cc

    sib = at(z, x, oc)
    xs = [x, lax.rem(x + 1, NX), lax.rem(x + 3, NX), lax.rem(x + 2, NX)]

    def zxor(d):
        if d == 1:
            return z + 1 - 2 * lax.rem(z, 2)
        if d == 2:
            return lax.rem(z + 2, 4)
        return 3 - z

    def remote(src, dst, ss, rs, seg_to):
        return pltpu.make_async_remote_copy(
            src_ref=src, dst_ref=dst, send_sem=ss, recv_sem=rs,
            device_id={"segment": seg_to}, device_id_type=MESH,
        )

    def send(src, dst, ss, rs, seg_to):
        cp = remote(src, dst, ss, rs, seg_to)
        cp.start()
        sends.append(cp)

    def wait_recv(dst, ss, rs):
        remote(dst, dst, ss, rs, sib).wait_recv()

    loads = [
        pltpu.make_async_copy(a, b, local_sem.at[i])
        for i, (a, b) in enumerate(
            [(h_hbm, h), (g_hbm, g), (tl_hbm, tl), (ids_hbm, ids), (wt_hbm, wt)]
        )
    ]
    for cp in loads:
        cp.start()
    wloads = [
        pltpu.make_async_copy(w_hbm.at[:, xs[i]], w.at[:, xs[i]], local_sem.at[5 + i])
        for i in range(NX)
    ]
    for cp in wloads:
        cp.start()
    barrier = pltpu.get_barrier_semaphore()
    partners = []
    for i in range(NX):
        for j in range(NC):
            if i or j:
                partners.append({"segment": at(z, xs[i], lax.rem(c + j, NC))})
    for d in (1, 2, 3):
        partners.append({"segment": at(zxor(d), x, c)})
    for d in range(1, ndp):
        partners.append({"dp": lax.rem(dpi + d, ndp)})
    for p in partners:
        pl.semaphore_signal(barrier, inc=1, device_id=p, device_id_type=MESH)

    loads[0].wait()
    loads[1].wait()
    grow = g[pl.ds(z * NX + x, 1), :]
    gcol[...] = jnp.transpose(jnp.broadcast_to(grow, (128, 128)))
    gown = gcol[pl.ds(c * FD, FD), :]
    hv = h[...]
    hg = hv * jnp.concatenate([gown] * (T // 128), axis=1)
    for b in range(NB):
        hb[b, z, x, c] = hg[:, b * TB : (b + 1) * TB].astype(BF16)
    sqrow = jnp.sum(hv * hv, axis=0, keepdims=True)
    slot = x * NC + c
    sq1[slot] = jnp.zeros((8, 128), F32)
    for r in range(T // 128):
        sq1[slot, r : r + 1, :] = sqrow[:, r * 128 : (r + 1) * 128]
    pl.semaphore_wait(barrier, len(partners))

    gath_count = [0] * NB

    def g_send(b, zz, xx, cc, seg_to):
        n = gath_count[b]
        gath_count[b] += 1
        ref = hb.at[b, zz, xx, cc]
        send(ref, ref, gath_s.at[b, n], gath_r.at[b, at(zz, xx, cc)], seg_to)

    def g_wait(b, zz, xx, cc):
        wait_recv(hb.at[b, zz, xx, cc], gath_s.at[b, 0], gath_r.at[b, at(zz, xx, cc)])

    def g_own(b):
        g_send(b, z, x, c, at(z, xs[1], c))
        g_send(b, z, x, c, at(z, xs[2], c))
        for d in (1, 3, 2):
            g_send(b, z, x, c, at(zxor(d), x, c))
        g_send(b, z, x, c, sib)

    def g_z(b, steps=(1, 3, 2)):
        for d in steps:
            zz = zxor(d)
            g_wait(b, zz, x, c)
            g_send(b, zz, x, c, at(z, xs[1], c))
            g_send(b, zz, x, c, at(z, xs[2], c))
            g_send(b, zz, x, c, sib)

    HR = FD // 2

    def g_half(b, zz, xx, j):
        return hb.at[b, zz, xx, c, pl.ds(j * HR, HR)]

    def g_half_sem(b, zz, xx, j):
        return gath_r.at[b, at(zz, xx, c) if j == 0 else 32 + zz]

    def g_x(b, steps=(0, 1, 3, 2)):
        for d in steps:
            zz = z if d == 0 else zxor(d)
            for j, (src, dst) in enumerate(((xs[2], xs[1]), (xs[1], xs[2]))):
                g_wait(b, zz, src, c)
                n = gath_count[b]
                gath_count[b] += 1
                ref = g_half(b, zz, src, j)
                send(ref, ref, gath_s.at[b, n], g_half_sem(b, zz, src, j), at(z, dst, c))
                g_send(b, zz, src, c, sib)

    def g_relay(b):
        for d in (0, 1, 3, 2):
            zz = z if d == 0 else zxor(d)
            for j in (0, 1):
                wait_recv(g_half(b, zz, xs[3], j), gath_s.at[b, 0], g_half_sem(b, zz, xs[3], j))
            g_send(b, zz, xs[3], c, sib)

    def l_col(b, i):
        xx = xs[i]
        for d in (0, 1, 2, 3):
            zz = z if d == 0 else zxor(d)
            g_wait(b, zz, xx, oc)
        if b == 0:
            wloads[i].wait()
        blk = hb[b, :, xx].reshape(NZ * NC * FD, TB)
        lhs[...] = jnp.transpose(blk)
        wt_ = w[:, xx].reshape(NZ * NC * FD, VS)
        r = jnp.dot(lhs[...], wt_, preferred_element_type=F32)
        if i == 0:
            logit[b] = r
            return
        r = r + logit[b]
        logit[b] = r
        if i == NX - 1:
            tops = [r[:, j * 128 : (j + 1) * 128] for j in range(VT)]
            stat[3] = functools.reduce(jnp.maximum, tops)

    def sq_first():
        n = 0
        for i in range(NX):
            for j in range(NC):
                if i or j:
                    ref = sq1.at[slot]
                    send(ref, ref, sq_s.at[n], sq_r.at[slot], at(z, xs[i], lax.rem(c + j, NC)))
                    n += 1

    def sq_second():
        for i in range(NX):
            for j in range(NC):
                if i or j:
                    s_ = xs[i] * NC + lax.rem(c + j, NC)
                    wait_recv(sq1.at[s_], sq_s.at[0], sq_r.at[s_])
        sq2[z] = jnp.sum(sq1[...], axis=0)
        for d in (1, 2, 3):
            ref = sq2.at[z]
            send(ref, ref, sq_s.at[6 + d], sq_r.at[8 + z], at(zxor(d), x, c))

    def to_cols(v, r, ref, row0):
        col = jnp.transpose(jnp.broadcast_to(v[r : r + 1, :], (128, 128)))
        ref[pl.ds(row0, 128), :] = col

    def sq_final():
        for d in (1, 2, 3):
            s_ = zxor(d)
            wait_recv(sq2.at[s_], sq_s.at[0], sq_r.at[8 + s_])
        inv = lax.rsqrt(jnp.sum(sq2[...], axis=0) / D + EPSILON)
        rows[0] = inv
        for r in range(T // 128):
            to_cols(inv, r, icol, r * 128)

    def teacher():
        loads[2].wait()
        loads[3].wait()
        t = tl[...]
        sh = t - jnp.max(t, axis=0, keepdims=True)
        logq = sh - jnp.log(jnp.sum(jnp.exp(sh), axis=0, keepdims=True))
        p = jnp.exp(logq)
        hrow = jnp.sum(p * logq, axis=0, keepdims=True)
        for r in range(T // 128):
            ent[r : r + 1, :] = hrow[:, r * 128 : (r + 1) * 128]
        local = ids[...] - seg * VS
        valid = (local >= 0) & (local < VS)
        hi = jnp.where(valid, lax.shift_right_logical(jnp.where(valid, local, 0), 7), -1)
        lo = jnp.where(valid, local, 0) & 127
        p1 = p.astype(BF16).astype(F32)
        p2 = p - p1
        allv = jnp.concatenate([hi.astype(F32), lo.astype(F32), p1, p2], axis=0)
        k = p.shape[0]
        cols = jnp.transpose(allv).astype(BF16)
        lane = lax.broadcasted_iota(jnp.int32, (4 * k, 8 * k), 1)
        row = lax.broadcasted_iota(jnp.int32, (4 * k, 8 * k), 0)
        lk = lane & (k - 1)
        tok = lax.broadcasted_iota(jnp.int32, (T, 8 * k), 0) & 7
        tl_lane = lax.shift_right_logical(
            lax.broadcasted_iota(jnp.int32, (T, 8 * k), 1), 5
        )
        own = tok == tl_lane
        for j, ref in enumerate((hi_x, lo_x, p1_x, p2_x)):
            pick = jnp.where(row == lk + j * k, 1.0, 0.0).astype(BF16)
            v = jnp.dot(cols, pick, preferred_element_type=F32)
            ref[...] = v if j == 0 else jnp.where(own, v, 0.0)

    def targets(b, lo_blk, hi_blk):
        sub = lax.broadcasted_iota(jnp.int32, (128, 256), 0).astype(F32).astype(BF16)
        half = (lax.broadcasted_iota(jnp.int32, (16, 256), 0) // 8).astype(F32).astype(BF16)
        nh = (VT + 1) // 2
        one, zero = jnp.ones((), BF16), jnp.zeros((), BF16)

        def twice(v):
            return jnp.concatenate([v, v], axis=0).astype(BF16)

        def body(n, carry):
            r0 = pl.multiple_of(b * TB + n * 8, 8)
            hx = twice(hi_x[pl.ds(r0, 8), :]) - half
            a1 = twice(p1_x[pl.ds(r0, 8), :])
            a2 = twice(p2_x[pl.ds(r0, 8), :])
            lrow = jnp.sum(lo_x[pl.ds(r0, 8), :], axis=0, keepdims=True).astype(BF16)
            bt = jnp.where(sub == lrow, one, zero)
            masks = [hx == jnp.asarray(2.0 * j, BF16) for j in range(nh)]
            a = jnp.concatenate(
                [jnp.where(m, a1, zero) for m in masks]
                + [jnp.where(m, a2, zero) for m in masks],
                axis=0,
            )
            o = lax.dot_general(a, bt, NT, preferred_element_type=F32)
            o = o[: 16 * nh] + o[16 * nh :]
            for j in range(VT):
                targ[b, pl.ds(pl.multiple_of(n * 8, 8), 8), j * 128 : (j + 1) * 128] = (
                    o[j * 8 : (j + 1) * 8]
                )
            return carry

        lax.fori_loop(lo_blk, hi_blk, body, 0, unroll=4)

    def softmax(b):
        R = 32
        tops = stat[3]
        for q in range(Q):
            tr = jnp.transpose(tops[q * 128 : (q + 1) * 128])
            mrow = jnp.max(tr, axis=0, keepdims=True)
            r = b * Q + q
            st1[b, slot, q : q + 1, :] = mrow * rows[0, r : r + 1, :]
        stat[3] = jnp.broadcast_to(jnp.max(tops, axis=1, keepdims=True), (TB, 128))

        def body(n, carry):
            r0 = pl.multiple_of(n * R, R)
            sc = icol[pl.ds(pl.multiple_of(b * TB + n * R, R), R), :] * LOG2E
            m = stat[3, pl.ds(r0, R), :]
            s = jnp.zeros((R, 128), F32)
            sl = jnp.zeros((R, 128), F32)
            pk = jnp.zeros((R, 128), F32)
            for j in range(VT):
                raw = logit[b, pl.ds(r0, R), j * 128 : (j + 1) * 128]
                e = jnp.exp2((raw - m) * sc)
                logit[b, pl.ds(r0, R), j * 128 : (j + 1) * 128] = e
                s += e
                sl += e * raw
                pk += targ[b, pl.ds(r0, R), j * 128 : (j + 1) * 128] * raw
            stat[0, pl.ds(r0, R), :] = s
            stat[1, pl.ds(r0, R), :] = sl
            stat[2, pl.ds(r0, R), :] = pk
            return carry

        lax.fori_loop(0, TB // R, body, 0, unroll=2)
        for q in range(Q):
            for k in range(3):
                tr = jnp.transpose(stat[k, q * 128 : (q + 1) * 128, :])
                r = (k + 1) * Q + q
                st1[b, slot, r : r + 1, :] = jnp.sum(tr, axis=0, keepdims=True)
        n = 0
        for i in range(NX):
            for j in range(NC):
                if i or j:
                    ref = st1.at[b, slot]
                    send(ref, ref, st_s.at[b, n], st_r.at[b, slot],
                         at(z, xs[i], lax.rem(c + j, NC)))
                    n += 1

    def merge(ref, b):
        m = ref[b, :, 0:Q, :]
        top = jnp.max(m, axis=0)
        wgt = jnp.exp(m - top[None])
        s = jnp.sum(wgt * ref[b, :, Q : 2 * Q, :], axis=0)
        sl = jnp.sum(wgt * ref[b, :, 2 * Q : 3 * Q, :], axis=0)
        pk = jnp.sum(ref[b, :, 3 * Q : 4 * Q, :], axis=0)
        return top, s, sl, pk

    def stat_second(b):
        for i in range(NX):
            for j in range(NC):
                if i or j:
                    s_ = xs[i] * NC + lax.rem(c + j, NC)
                    wait_recv(st1.at[b, s_], st_s.at[b, 0], st_r.at[b, s_])
        for k, v in enumerate(merge(st1, b)):
            st2[b, z, k * Q : (k + 1) * Q, :] = v
        for d in (1, 2, 3):
            ref = st2.at[b, z]
            send(ref, ref, st_s.at[b, 6 + d], st_r.at[b, 8 + z], at(zxor(d), x, c))

    def stat_final(b):
        for d in (1, 2, 3):
            s_ = zxor(d)
            wait_recv(st2.at[b, s_], st_s.at[b, 0], st_r.at[b, 8 + s_])
        top, s, sl, pk = merge(st2, b)
        total = top + jnp.log(s)
        inv = rows[0, b * Q : (b + 1) * Q, :]
        lossv[b * Q : (b + 1) * Q, :] = ent[b * Q : (b + 1) * Q, :] - inv * pk + total
        rows[1, b * Q : (b + 1) * Q, :] = sl / s - pk
        scale = jnp.exp(st1[b, slot, 0:Q, :] - total)
        for q in range(Q):
            to_cols(scale, q, acol, q * 128)

    def make_gl(b):
        def body(n, carry):
            r0 = pl.multiple_of(n * 16, 16)
            a = acol[pl.ds(r0, 16), :]
            for j in range(VT):
                sl_ = slice(j * 128, (j + 1) * 128)
                gl[pl.ds(r0, 16), sl_] = (
                    logit[b, pl.ds(r0, 16), sl_] * a - targ[b, pl.ds(r0, 16), sl_]
                ).astype(BF16)
            return carry

        lax.fori_loop(0, TB // 16, body, 0)

    order = [3, 1, 2, 0]

    def mm(b, k):
        xx = xs[order[k]]
        wt_ = w[:, xx].reshape(NZ * NC * FD, VS)
        r = lax.dot_general(wt_, gl[...], NT, preferred_element_type=F32)
        gs[b, k] = r.reshape(NZ, NC, FD, TB)
        sib_s[b, k] = gs[b, k, :, oc].astype(BF16)
        send(sib_s.at[b, k], sib_r.at[b, k], rs_s.at[b, k], rs_r.at[b, k], sib)

    def pair(b, k):
        wait_recv(sib_r.at[b, k], rs_s.at[b, 0], rs_r.at[b, k])
        return gs[b, k, :, c] + sib_r[b, k].astype(F32)

    def rs_col(b, k):
        v = pair(b, k)
        if k == 0:
            for j in (0, 1):
                rl_s[b, j] = v[:, j * HR : (j + 1) * HR].astype(BF16)
            for d in (1, 3, 2, 0):
                zz = z if d == 0 else zxor(d)
                for j in (0, 1):
                    n = 4 + 4 * j + zz
                    send(rl_s.at[b, j, zz], rl_r.at[b, j, zz], rs_s.at[b, n], rs_r.at[b, n],
                         at(z, xs[1 + j], c))
            return
        gs[b, k, :, 0] = v
        if k in (1, 2):
            j = k - 1
            for d in (1, 3, 2, 0):
                zz = z if d == 0 else zxor(d)
                wait_recv(rl_r.at[b, j, zz], rs_s.at[b, 0], rs_r.at[b, 4 + 4 * j + zz])
                u = gs[b, k, zz, 0]
                part = u[j * HR : (j + 1) * HR] + rl_r[b, j, zz].astype(F32)
                rest = u[(1 - j) * HR : (2 - j) * HR]
                dr_s[b, j, zz] = jnp.concatenate(
                    [part, rest] if j == 0 else [rest, part], axis=0
                ).astype(BF16)
                n = 12 + 4 * j + zz
                send(dr_s.at[b, j, zz], dr_r.at[b, j, zz], rs_s.at[b, n], rs_r.at[b, n],
                     at(z, xs[k], c))
            return
        for d in (1, 3, 2, 0):
            zz = z if d == 0 else zxor(d)
            for j in (0, 1):
                wait_recv(dr_r.at[b, j, zz], rs_s.at[b, 0], rs_r.at[b, 12 + 4 * j + zz])
            u = gs[b, 3, zz, 0] + dr_r[b, 0, zz].astype(F32) + dr_r[b, 1, zz].astype(F32)
            if d:
                z_s[b, zz] = u.astype(BF16)
                send(z_s.at[b, zz], z_r.at[b, z], rs_s.at[b, 19 + d], rs_r.at[b, 20 + z],
                     at(zz, x, c))
            else:
                gradv[:, b * TB : (b + 1) * TB] = u

    def row_of(v, b):
        return jnp.concatenate([v[b * Q + q : b * Q + q + 1, :] for q in range(Q)], axis=1)

    def finish(b):
        cols = slice(b * TB, (b + 1) * TB)
        tot = gradv[:, cols]
        for d in (1, 2, 3):
            s_ = zxor(d)
            wait_recv(z_r.at[b, s_], rs_s.at[b, 0], rs_r.at[b, 20 + s_])
            tot = tot + z_r[b, s_].astype(F32)
        inv = rows[0]
        first = row_of(inv * rows[2], b)
        second = row_of(inv * inv * rows[1] / D, b)
        gn = jnp.concatenate([gcol[pl.ds(c * FD, FD), :]] * Q, axis=1)
        gradv[:, cols] = first * (gn * tot - h[:, cols] * second)

    def dp_send():
        wv = wt[...]
        lane_sum = lambda v: jnp.sum(jnp.sum(v, axis=1, keepdims=True), axis=0, keepdims=True)
        dps[dpi] = jnp.zeros((8, 128), F32)
        dps[dpi, 0:1, :] = jnp.broadcast_to(lane_sum(wv), (1, 128))
        dps[dpi, 1:2, :] = jnp.broadcast_to(lane_sum(wv * lossv[...]), (1, 128))
        for d in range(1, ndp):
            cp = pltpu.make_async_remote_copy(
                src_ref=dps.at[dpi], dst_ref=dps.at[dpi], send_sem=dp_s.at[d],
                recv_sem=dp_r.at[dpi], device_id={"dp": lax.rem(dpi + d, ndp)},
                device_id_type=MESH,
            )
            cp.start()
            sends.append(cp)

    def dp_final():
        for d in range(1, ndp):
            s_ = lax.rem(dpi + d, ndp)
            wait_recv(dps.at[s_], dp_s.at[0], dp_r.at[s_])
        tot = jnp.sum(dps[...], axis=0)
        meanv[...] = jnp.broadcast_to(tot[1:2, :] / tot[0:1, :], meanv.shape)
        rows[2, 0 : T // 128, :] = wt[...] * tokens / tot[0:1, :]

    nblk = TB // 8
    if NB == 1:
        part = nblk // 8
        g_own(0)
        sq_first()
        teacher()
        targets(0, 0, 2 * part)
        g_z(0, (1,))
        g_x(0, (0,))
        targets(0, 2 * part, 4 * part)
        g_z(0, (3,))
        sq_second()
        g_x(0, (1,))
        g_z(0, (2,))
        targets(0, 4 * part, 6 * part)
        g_x(0, (3,))
        l_col(0, 0)
        g_x(0, (2,))
        targets(0, 6 * part, nblk)
        l_col(0, 1)
        sq_final()
        g_relay(0)
        l_col(0, 2)
        l_col(0, 3)
        softmax(0)
        loads[4].wait()
        stat_second(0)
        stat_final(0)
        make_gl(0)
        mm(0, 0)
        mm(0, 1)
        rs_col(0, 0)
        mm(0, 2)
        rs_col(0, 1)
        rs_col(0, 2)
        dp_send()
        mm(0, 3)
        dp_final()
        rs_col(0, 3)
        finish(0)
    else:
        part = nblk // 4
        g_own(0)
        sq_first()
        g_own(1)
        teacher()
        targets(0, 0, 2 * part)
        g_z(0, (1,))
        g_x(0, (0,))
        targets(0, 2 * part, 3 * part)
        g_x(1, (0,))
        g_z(1, (1,))
        targets(0, 3 * part, nblk)
        sq_second()
        g_z(0, (3, 2))
        g_x(0, (1,))
        targets(1, 0, 2 * part)
        g_z(1, (3, 2))
        targets(1, 2 * part, 3 * part)
        g_x(0, (3, 2))
        l_col(0, 0)
        g_x(1, (1,))
        targets(1, 3 * part, nblk)
        g_relay(0)
        l_col(0, 1)
        g_x(1, (3, 2))
        l_col(0, 2)
        sq_final()
        l_col(0, 3)
        softmax(0)
        l_col(1, 0)
        g_relay(1)
        l_col(1, 1)
        l_col(1, 2)
        stat_second(0)
        l_col(1, 3)
        softmax(1)
        stat_final(0)
        make_gl(0)
        mm(0, 0)
        mm(0, 1)
        rs_col(0, 0)
        stat_second(1)
        mm(0, 2)
        mm(0, 3)
        rs_col(0, 1)
        rs_col(0, 2)
        stat_final(1)
        make_gl(1)
        loads[4].wait()
        mm(1, 0)
        mm(1, 1)
        rs_col(1, 0)
        dp_send()
        mm(1, 2)
        mm(1, 3)
        rs_col(1, 1)
        rs_col(1, 2)
        rs_col(0, 3)
        dp_final()
        finish(0)
        rs_col(1, 3)
        finish(1)

    outs = [
        pltpu.make_async_copy(a, b, local_sem.at[9 + i])
        for i, (a, b) in enumerate([(lossv, loss_out), (meanv, mean_out), (gradv, grad_out)])
    ]
    for cp in outs:
        cp.start()
    for cp in sends:
        cp.wait_send()
    for cp in outs:
        cp.wait()


NB_TOKENS = 1


def write_out(loss, mean, grad, loss_out, mean_out, grad_out):
    loss_out[...] = loss[...]
    mean_out[...] = mean[0:1, 0:1]
    grad_out[...] = grad[...]


def shards(hidden_rows, norm_gain, head_weight, teacher_ids, teacher_logits, token_weights):
    T, FD = hidden_rows.shape
    VS = head_weight.shape[1]
    K = teacher_ids.shape[1]
    ndp = lax.axis_size("dp")
    NB = NB_TOKENS
    TB = T // NB
    Q = TB // 128
    any_ = pl.BlockSpec(memory_space=pl.ANY)
    V = pltpu.VMEM
    dma = pltpu.SemaphoreType.DMA
    scratch = [
        V((FD, T), F32), V((NZ * NX, 128), F32), V((NZ, NX, NC * FD, VS), BF16),
        V((K, T), jnp.int32), V((K, T), F32), V((T // 128, 128), F32),
        V((128, 128), F32),
        V((NB, NZ, NX, NC, FD, TB), BF16),
        V((TB, NZ * NC * FD), BF16),
        V((NB, TB, VS), F32),
        V((NB, TB, VS), F32),
        V((TB, VS), BF16),
        V((T, 8 * K), F32), V((T, 8 * K), F32), V((T, 8 * K), F32), V((T, 8 * K), F32),
        V((T, 128), F32), V((TB, 128), F32), V((4, TB, 128), F32),
        V((NX * NC, 8, 128), F32), V((NZ, 8, 128), F32),
        V((NB, NX * NC, 4 * Q, 128), F32), V((NB, NZ, 4 * Q, 128), F32),
        V((ndp, 8, 128), F32), V((T // 128, 128), F32), V((3, 8, 128), F32),
        V((NB, 4, NZ, NC, FD, TB), F32),
        V((NB, 4, NZ, FD, TB), BF16), V((NB, 4, NZ, FD, TB), BF16),
        V((NB, 2, NZ, FD // 2, TB), BF16), V((NB, 2, NZ, FD // 2, TB), BF16),
        V((NB, 2, NZ, FD, TB), BF16), V((NB, 2, NZ, FD, TB), BF16),
        V((NB, NZ, FD, TB), BF16), V((NB, NZ, FD, TB), BF16),
        V((T // 128, 128), F32), V((8, 128), F32), V((FD, T), F32),
        dma((12,)), dma((NB, 36)), dma((NB, 35)), dma((12,)), dma((10,)),
        dma((NB, 12)), dma((NB, 10)), dma((ndp,)), dma((ndp,)), dma((NB, 24)), dma((NB, 23)),
    ]
    loss, mean, grad = pl.pallas_call(
        functools.partial(kernel, (NB, TB, VS, ndp, T * ndp)),
        out_shape=(
            jax.ShapeDtypeStruct((T // 128, 128), F32),
            jax.ShapeDtypeStruct((8, 128), F32),
            jax.ShapeDtypeStruct((FD, T), F32),
        ),
        in_specs=[any_] * 6,
        out_specs=(any_, any_, any_),
        scratch_shapes=scratch,
        compiler_params=pltpu.CompilerParams(
            collective_id=0, has_side_effects=True, vmem_limit_bytes=60 * 1024 * 1024
        ),
    )(
        hidden_rows.T,
        norm_gain.reshape(NZ * NX, 128),
        head_weight.reshape(NZ, NX, NC * FD, VS),
        teacher_ids.T,
        teacher_logits.T,
        token_weights.reshape(T // 128, 128),
    )
    loss, mean, grad = pl.pallas_call(
        write_out,
        out_shape=(
            jax.ShapeDtypeStruct((T // 128, 128), F32),
            jax.ShapeDtypeStruct((1, 1), F32),
            jax.ShapeDtypeStruct((FD, T), F32),
        ),
    )(loss, mean, grad)
    return (loss.reshape(T), mean.reshape(()), grad.T)


def solution(mesh):
    in_specs = (P("dp", "segment"), P(), P(None, "segment"), P("dp", None), P("dp", None), P("dp"))
    out_specs = (P("dp"), P(), P("dp", "segment"))
    return jax.shard_map(shards, mesh=mesh, in_specs=in_specs, out_specs=out_specs, check_vma=False)
```

```python
import functools

import jax
import jax.numpy as jnp
from jax import lax
from jax.experimental import pallas as pl
from jax.experimental.pallas import tpu as pltpu
from jax.sharding import PartitionSpec as P

D = 2048
EPSILON = 1e-06
NZ, NX, NC = 4, 4, 2
LOG2E = 1.4426950408889634
NT = (((1,), (1,)), ((), ()))
MESH = pl.DeviceIdType.MESH
F32, BF16 = jnp.float32, jnp.bfloat16


def kernel(
    cfg,
    h_hbm, g_hbm, w_hbm, ids_hbm, tl_hbm, wt_hbm,
    loss_out, mean_out, grad_out,
    h, g, w, ids, tl, wt,
    gcol, hb, lhs, logit, targ, gl, hi_x, lo_x, p1_x, p2_x,
    icol, acol, stat, sq1, sq2, st1, st2, dps, ent, rows,
    gs, sib_s, sib_r, rl_s, rl_r, dr_s, dr_r, z_s, z_r,
    lossv, meanv, gradv,
    local_sem, gath_r, gath_s, sq_r, sq_s, st_r, st_s, dp_r, dp_s, rs_r, rs_s,
):
    NB, TB, VS, ndp, tokens = cfg
    T = NB * TB
    Q = TB // 128
    FD = D // (NZ * NX * NC)
    VT = VS // 128
    seg = lax.axis_index("segment")
    dpi = lax.axis_index("dp")
    c = lax.rem(seg, NC)
    x = lax.rem(lax.div(seg, NC), NX)
    z = lax.div(seg, NC * NX)
    oc = 1 - c
    sends = []

    def at(zz, xx, cc):
        return (zz * NX + xx) * NC + cc

    sib = at(z, x, oc)
    xs = [x, lax.rem(x + 1, NX), lax.rem(x + 3, NX), lax.rem(x + 2, NX)]

    def zxor(d):
        if d == 1:
            return z + 1 - 2 * lax.rem(z, 2)
        if d == 2:
            return lax.rem(z + 2, 4)
        return 3 - z

    def remote(src, dst, ss, rs, seg_to):
        return pltpu.make_async_remote_copy(
            src_ref=src, dst_ref=dst, send_sem=ss, recv_sem=rs,
            device_id={"segment": seg_to}, device_id_type=MESH,
        )

    def send(src, dst, ss, rs, seg_to):
        cp = remote(src, dst, ss, rs, seg_to)
        cp.start()
        sends.append(cp)

    def wait_recv(dst, ss, rs):
        remote(dst, dst, ss, rs, sib).wait_recv()

    loads = [
        pltpu.make_async_copy(a, b, local_sem.at[i])
        for i, (a, b) in enumerate(
            [(h_hbm, h), (g_hbm, g), (tl_hbm, tl), (ids_hbm, ids), (wt_hbm, wt)]
        )
    ]
    for cp in loads:
        cp.start()
    wloads = [
        pltpu.make_async_copy(w_hbm.at[:, xs[i]], w.at[:, xs[i]], local_sem.at[5 + i])
        for i in range(NX)
    ]
    for cp in wloads:
        cp.start()
    barrier = pltpu.get_barrier_semaphore()
    partners = []
    for i in range(NX):
        for j in range(NC):
            if i or j:
                partners.append({"segment": at(z, xs[i], lax.rem(c + j, NC))})
    for d in (1, 2, 3):
        partners.append({"segment": at(zxor(d), x, c)})
    for d in range(1, ndp):
        partners.append({"dp": lax.rem(dpi + d, ndp)})
    for p in partners:
        pl.semaphore_signal(barrier, inc=1, device_id=p, device_id_type=MESH)

    loads[0].wait()
    loads[1].wait()
    grow = g[pl.ds(z * NX + x, 1), :]
    gcol[...] = jnp.transpose(jnp.broadcast_to(grow, (128, 128)))
    gown = gcol[pl.ds(c * FD, FD), :]
    hv = h[...]
    hg = hv * jnp.concatenate([gown] * (T // 128), axis=1)
    for b in range(NB):
        hb[b, z, x, c] = hg[:, b * TB : (b + 1) * TB].astype(BF16)
    sqrow = jnp.sum(hv * hv, axis=0, keepdims=True)
    slot = x * NC + c
    sq1[slot] = jnp.zeros((8, 128), F32)
    for r in range(T // 128):
        sq1[slot, r : r + 1, :] = sqrow[:, r * 128 : (r + 1) * 128]
    pl.semaphore_wait(barrier, len(partners))

    gath_count = [0] * NB

    def g_send(b, zz, xx, cc, seg_to):
        n = gath_count[b]
        gath_count[b] += 1
        ref = hb.at[b, zz, xx, cc]
        send(ref, ref, gath_s.at[b, n], gath_r.at[b, at(zz, xx, cc)], seg_to)

    def g_wait(b, zz, xx, cc):
        wait_recv(hb.at[b, zz, xx, cc], gath_s.at[b, 0], gath_r.at[b, at(zz, xx, cc)])

    def g_own(b):
        g_send(b, z, x, c, at(z, xs[1], c))
        g_send(b, z, x, c, at(z, xs[2], c))
        for d in (1, 3, 2):
            g_send(b, z, x, c, at(zxor(d), x, c))
        g_send(b, z, x, c, sib)

    def g_z(b, steps=(1, 3, 2)):
        for d in steps:
            zz = zxor(d)
            g_wait(b, zz, x, c)
            g_send(b, zz, x, c, at(z, xs[1], c))
            g_send(b, zz, x, c, at(z, xs[2], c))
            g_send(b, zz, x, c, sib)

    HR = FD // 2

    def g_half(b, zz, xx, j):
        return hb.at[b, zz, xx, c, pl.ds(j * HR, HR)]

    def g_half_sem(b, zz, xx, j):
        return gath_r.at[b, at(zz, xx, c) if j == 0 else 32 + zz]

    def g_x(b, steps=(0, 1, 3, 2)):
        for d in steps:
            zz = z if d == 0 else zxor(d)
            for j, (src, dst) in enumerate(((xs[2], xs[1]), (xs[1], xs[2]))):
                g_wait(b, zz, src, c)
                n = gath_count[b]
                gath_count[b] += 1
                ref = g_half(b, zz, src, j)
                send(ref, ref, gath_s.at[b, n], g_half_sem(b, zz, src, j), at(z, dst, c))
                g_send(b, zz, src, c, sib)

    def g_relay(b):
        for d in (0, 1, 3, 2):
            zz = z if d == 0 else zxor(d)
            for j in (0, 1):
                wait_recv(g_half(b, zz, xs[3], j), gath_s.at[b, 0], g_half_sem(b, zz, xs[3], j))
            g_send(b, zz, xs[3], c, sib)

    def l_col(b, i):
        xx = xs[i]
        for d in (0, 1, 2, 3):
            zz = z if d == 0 else zxor(d)
            g_wait(b, zz, xx, oc)
        if b == 0:
            wloads[i].wait()
        blk = hb[b, :, xx].reshape(NZ * NC * FD, TB)
        lhs[...] = jnp.transpose(blk)
        wt_ = w[:, xx].reshape(NZ * NC * FD, VS)
        r = jnp.dot(lhs[...], wt_, preferred_element_type=F32)
        if i == 0:
            logit[b] = r
            return
        r = r + logit[b]
        logit[b] = r
        if i == NX - 1:
            tops = [r[:, j * 128 : (j + 1) * 128] for j in range(VT)]
            stat[3] = functools.reduce(jnp.maximum, tops)

    def sq_first():
        n = 0
        for i in range(NX):
            for j in range(NC):
                if i or j:
                    ref = sq1.at[slot]
                    send(ref, ref, sq_s.at[n], sq_r.at[slot], at(z, xs[i], lax.rem(c + j, NC)))
                    n += 1

    def sq_second():
        for i in range(NX):
            for j in range(NC):
                if i or j:
                    s_ = xs[i] * NC + lax.rem(c + j, NC)
                    wait_recv(sq1.at[s_], sq_s.at[0], sq_r.at[s_])
        sq2[z] = jnp.sum(sq1[...], axis=0)
        for d in (1, 2, 3):
            ref = sq2.at[z]
            send(ref, ref, sq_s.at[6 + d], sq_r.at[8 + z], at(zxor(d), x, c))

    def to_cols(v, r, ref, row0):
        col = jnp.transpose(jnp.broadcast_to(v[r : r + 1, :], (128, 128)))
        ref[pl.ds(row0, 128), :] = col

    def sq_final():
        for d in (1, 2, 3):
            s_ = zxor(d)
            wait_recv(sq2.at[s_], sq_s.at[0], sq_r.at[8 + s_])
        inv = lax.rsqrt(jnp.sum(sq2[...], axis=0) / D + EPSILON)
        rows[0] = inv
        for r in range(T // 128):
            to_cols(inv, r, icol, r * 128)

    def teacher():
        loads[2].wait()
        loads[3].wait()
        t = tl[...]
        sh = t - jnp.max(t, axis=0, keepdims=True)
        logq = sh - jnp.log(jnp.sum(jnp.exp(sh), axis=0, keepdims=True))
        p = jnp.exp(logq)
        hrow = jnp.sum(p * logq, axis=0, keepdims=True)
        for r in range(T // 128):
            ent[r : r + 1, :] = hrow[:, r * 128 : (r + 1) * 128]
        local = ids[...] - seg * VS
        valid = (local >= 0) & (local < VS)
        hi = jnp.where(valid, lax.shift_right_logical(jnp.where(valid, local, 0), 7), -1)
        lo = jnp.where(valid, local, 0) & 127
        p1 = p.astype(BF16).astype(F32)
        p2 = p - p1
        allv = jnp.concatenate([hi.astype(F32), lo.astype(F32), p1, p2], axis=0)
        k = p.shape[0]
        cols = jnp.transpose(allv).astype(BF16)
        lane = lax.broadcasted_iota(jnp.int32, (4 * k, 8 * k), 1)
        row = lax.broadcasted_iota(jnp.int32, (4 * k, 8 * k), 0)
        lk = lane & (k - 1)
        tok = lax.broadcasted_iota(jnp.int32, (T, 8 * k), 0) & 7
        tl_lane = lax.shift_right_logical(
            lax.broadcasted_iota(jnp.int32, (T, 8 * k), 1), 5
        )
        own = tok == tl_lane
        for j, ref in enumerate((hi_x, lo_x, p1_x, p2_x)):
            pick = jnp.where(row == lk + j * k, 1.0, 0.0).astype(BF16)
            v = jnp.dot(cols, pick, preferred_element_type=F32)
            ref[...] = v if j == 0 else jnp.where(own, v, 0.0)

    def targets(b, lo_blk, hi_blk):
        sub = lax.broadcasted_iota(jnp.int32, (128, 256), 0).astype(F32).astype(BF16)
        half = (lax.broadcasted_iota(jnp.int32, (16, 256), 0) // 8).astype(F32).astype(BF16)
        nh = (VT + 1) // 2
        one, zero = jnp.ones((), BF16), jnp.zeros((), BF16)

        def twice(v):
            return jnp.concatenate([v, v], axis=0).astype(BF16)

        def body(n, carry):
            r0 = pl.multiple_of(b * TB + n * 8, 8)
            hx = twice(hi_x[pl.ds(r0, 8), :]) - half
            a1 = twice(p1_x[pl.ds(r0, 8), :])
            a2 = twice(p2_x[pl.ds(r0, 8), :])
            lrow = jnp.sum(lo_x[pl.ds(r0, 8), :], axis=0, keepdims=True).astype(BF16)
            bt = jnp.where(sub == lrow, one, zero)
            masks = [hx == jnp.asarray(2.0 * j, BF16) for j in range(nh)]
            a = jnp.concatenate(
                [jnp.where(m, a1, zero) for m in masks]
                + [jnp.where(m, a2, zero) for m in masks],
                axis=0,
            )
            o = lax.dot_general(a, bt, NT, preferred_element_type=F32)
            o = o[: 16 * nh] + o[16 * nh :]
            for j in range(VT):
                targ[b, pl.ds(pl.multiple_of(n * 8, 8), 8), j * 128 : (j + 1) * 128] = (
                    o[j * 8 : (j + 1) * 8]
                )
            return carry

        lax.fori_loop(lo_blk, hi_blk, body, 0, unroll=4)

    def softmax(b):
        R = 32
        tops = stat[3]
        for q in range(Q):
            tr = jnp.transpose(tops[q * 128 : (q + 1) * 128])
            mrow = jnp.max(tr, axis=0, keepdims=True)
            r = b * Q + q
            st1[b, slot, q : q + 1, :] = mrow * rows[0, r : r + 1, :]
        stat[3] = jnp.broadcast_to(jnp.max(tops, axis=1, keepdims=True), (TB, 128))

        def body(n, carry):
            r0 = pl.multiple_of(n * R, R)
            sc = icol[pl.ds(pl.multiple_of(b * TB + n * R, R), R), :] * LOG2E
            m = stat[3, pl.ds(r0, R), :]
            s = jnp.zeros((R, 128), F32)
            sl = jnp.zeros((R, 128), F32)
            pk = jnp.zeros((R, 128), F32)
            for j in range(VT):
                raw = logit[b, pl.ds(r0, R), j * 128 : (j + 1) * 128]
                e = jnp.exp2((raw - m) * sc)
                logit[b, pl.ds(r0, R), j * 128 : (j + 1) * 128] = e
                s += e
                sl += e * raw
                pk += targ[b, pl.ds(r0, R), j * 128 : (j + 1) * 128] * raw
            stat[0, pl.ds(r0, R), :] = s
            stat[1, pl.ds(r0, R), :] = sl
            stat[2, pl.ds(r0, R), :] = pk
            return carry

        lax.fori_loop(0, TB // R, body, 0, unroll=2)
        for q in range(Q):
            for k in range(3):
                tr = jnp.transpose(stat[k, q * 128 : (q + 1) * 128, :])
                r = (k + 1) * Q + q
                st1[b, slot, r : r + 1, :] = jnp.sum(tr, axis=0, keepdims=True)
        n = 0
        for i in range(NX):
            for j in range(NC):
                if i or j:
                    ref = st1.at[b, slot]
                    send(ref, ref, st_s.at[b, n], st_r.at[b, slot],
                         at(z, xs[i], lax.rem(c + j, NC)))
                    n += 1

    def merge(ref, b):
        m = ref[b, :, 0:Q, :]
        top = jnp.max(m, axis=0)
        wgt = jnp.exp(m - top[None])
        s = jnp.sum(wgt * ref[b, :, Q : 2 * Q, :], axis=0)
        sl = jnp.sum(wgt * ref[b, :, 2 * Q : 3 * Q, :], axis=0)
        pk = jnp.sum(ref[b, :, 3 * Q : 4 * Q, :], axis=0)
        return top, s, sl, pk

    def stat_second(b):
        for i in range(NX):
            for j in range(NC):
                if i or j:
                    s_ = xs[i] * NC + lax.rem(c + j, NC)
                    wait_recv(st1.at[b, s_], st_s.at[b, 0], st_r.at[b, s_])
        for k, v in enumerate(merge(st1, b)):
            st2[b, z, k * Q : (k + 1) * Q, :] = v
        for d in (1, 2, 3):
            ref = st2.at[b, z]
            send(ref, ref, st_s.at[b, 6 + d], st_r.at[b, 8 + z], at(zxor(d), x, c))

    def stat_final(b):
        for d in (1, 2, 3):
            s_ = zxor(d)
            wait_recv(st2.at[b, s_], st_s.at[b, 0], st_r.at[b, 8 + s_])
        top, s, sl, pk = merge(st2, b)
        total = top + jnp.log(s)
        inv = rows[0, b * Q : (b + 1) * Q, :]
        lossv[b * Q : (b + 1) * Q, :] = ent[b * Q : (b + 1) * Q, :] - inv * pk + total
        rows[1, b * Q : (b + 1) * Q, :] = sl / s - pk
        scale = jnp.exp(st1[b, slot, 0:Q, :] - total)
        for q in range(Q):
            to_cols(scale, q, acol, q * 128)

    def make_gl(b):
        def body(n, carry):
            r0 = pl.multiple_of(n * 16, 16)
            a = acol[pl.ds(r0, 16), :]
            for j in range(VT):
                sl_ = slice(j * 128, (j + 1) * 128)
                gl[pl.ds(r0, 16), sl_] = (
                    logit[b, pl.ds(r0, 16), sl_] * a - targ[b, pl.ds(r0, 16), sl_]
                ).astype(BF16)
            return carry

        lax.fori_loop(0, TB // 16, body, 0)

    order = [3, 1, 2, 0]

    def mm(b, k):
        xx = xs[order[k]]
        wt_ = w[:, xx].reshape(NZ * NC * FD, VS)
        r = lax.dot_general(wt_, gl[...], NT, preferred_element_type=F32)
        gs[b, k] = r.reshape(NZ, NC, FD, TB)
        sib_s[b, k] = gs[b, k, :, oc].astype(BF16)
        send(sib_s.at[b, k], sib_r.at[b, k], rs_s.at[b, k], rs_r.at[b, k], sib)

    def pair(b, k):
        wait_recv(sib_r.at[b, k], rs_s.at[b, 0], rs_r.at[b, k])
        return gs[b, k, :, c] + sib_r[b, k].astype(F32)

    def rs_col(b, k):
        v = pair(b, k)
        if k == 0:
            for j in (0, 1):
                rl_s[b, j] = v[:, j * HR : (j + 1) * HR].astype(BF16)
            for d in (1, 3, 2, 0):
                zz = z if d == 0 else zxor(d)
                for j in (0, 1):
                    n = 4 + 4 * j + zz
                    send(rl_s.at[b, j, zz], rl_r.at[b, j, zz], rs_s.at[b, n], rs_r.at[b, n],
                         at(z, xs[1 + j], c))
            return
        gs[b, k, :, 0] = v
        if k in (1, 2):
            j = k - 1
            for d in (1, 3, 2, 0):
                zz = z if d == 0 else zxor(d)
                wait_recv(rl_r.at[b, j, zz], rs_s.at[b, 0], rs_r.at[b, 4 + 4 * j + zz])
                u = gs[b, k, zz, 0]
                part = u[j * HR : (j + 1) * HR] + rl_r[b, j, zz].astype(F32)
                rest = u[(1 - j) * HR : (2 - j) * HR]
                dr_s[b, j, zz] = jnp.concatenate(
                    [part, rest] if j == 0 else [rest, part], axis=0
                ).astype(BF16)
                n = 12 + 4 * j + zz
                send(dr_s.at[b, j, zz], dr_r.at[b, j, zz], rs_s.at[b, n], rs_r.at[b, n],
                     at(z, xs[k], c))
            return
        for d in (1, 3, 2, 0):
            zz = z if d == 0 else zxor(d)
            for j in (0, 1):
                wait_recv(dr_r.at[b, j, zz], rs_s.at[b, 0], rs_r.at[b, 12 + 4 * j + zz])
            u = gs[b, 3, zz, 0] + dr_r[b, 0, zz].astype(F32) + dr_r[b, 1, zz].astype(F32)
            if d:
                z_s[b, zz] = u.astype(BF16)
                send(z_s.at[b, zz], z_r.at[b, z], rs_s.at[b, 19 + d], rs_r.at[b, 20 + z],
                     at(zz, x, c))
            else:
                gradv[:, b * TB : (b + 1) * TB] = u

    def row_of(v, b):
        return jnp.concatenate([v[b * Q + q : b * Q + q + 1, :] for q in range(Q)], axis=1)

    def finish(b):
        cols = slice(b * TB, (b + 1) * TB)
        tot = gradv[:, cols]
        for d in (1, 2, 3):
            s_ = zxor(d)
            wait_recv(z_r.at[b, s_], rs_s.at[b, 0], rs_r.at[b, 20 + s_])
            tot = tot + z_r[b, s_].astype(F32)
        inv = rows[0]
        first = row_of(inv * rows[2], b)
        second = row_of(inv * inv * rows[1] / D, b)
        gn = jnp.concatenate([gcol[pl.ds(c * FD, FD), :]] * Q, axis=1)
        gradv[:, cols] = first * (gn * tot - h[:, cols] * second)

    def dp_send():
        wv = wt[...]
        lane_sum = lambda v: jnp.sum(jnp.sum(v, axis=1, keepdims=True), axis=0, keepdims=True)
        dps[dpi] = jnp.zeros((8, 128), F32)
        dps[dpi, 0:1, :] = jnp.broadcast_to(lane_sum(wv), (1, 128))
        dps[dpi, 1:2, :] = jnp.broadcast_to(lane_sum(wv * lossv[...]), (1, 128))
        for d in range(1, ndp):
            cp = pltpu.make_async_remote_copy(
                src_ref=dps.at[dpi], dst_ref=dps.at[dpi], send_sem=dp_s.at[d],
                recv_sem=dp_r.at[dpi], device_id={"dp": lax.rem(dpi + d, ndp)},
                device_id_type=MESH,
            )
            cp.start()
            sends.append(cp)

    def dp_final():
        for d in range(1, ndp):
            s_ = lax.rem(dpi + d, ndp)
            wait_recv(dps.at[s_], dp_s.at[0], dp_r.at[s_])
        tot = jnp.sum(dps[...], axis=0)
        meanv[...] = jnp.broadcast_to(tot[1:2, :] / tot[0:1, :], meanv.shape)
        rows[2, 0 : T // 128, :] = wt[...] * tokens / tot[0:1, :]

    nblk = TB // 8
    if NB == 1:
        part = nblk // 8
        g_own(0)
        sq_first()
        teacher()
        targets(0, 0, 2 * part)
        g_z(0, (1,))
        g_x(0, (0,))
        targets(0, 2 * part, 4 * part)
        g_z(0, (3,))
        sq_second()
        g_x(0, (1,))
        g_z(0, (2,))
        targets(0, 4 * part, 6 * part)
        g_x(0, (3,))
        targets(0, 6 * part, nblk)
        g_x(0, (2,))
        l_col(0, 0)
        l_col(0, 1)
        sq_final()
        g_relay(0)
        l_col(0, 2)
        l_col(0, 3)
        softmax(0)
        loads[4].wait()
        stat_second(0)
        stat_final(0)
        make_gl(0)
        mm(0, 0)
        mm(0, 1)
        rs_col(0, 0)
        mm(0, 2)
        rs_col(0, 1)
        rs_col(0, 2)
        dp_send()
        mm(0, 3)
        dp_final()
        rs_col(0, 3)
        finish(0)
    else:
        part = nblk // 4
        g_own(0)
        sq_first()
        g_own(1)
        teacher()
        targets(0, 0, 2 * part)
        g_z(0, (1,))
        g_x(0, (0,))
        targets(0, 2 * part, 3 * part)
        g_x(1, (0,))
        g_z(1, (1,))
        targets(0, 3 * part, nblk)
        sq_second()
        g_z(0, (3, 2))
        g_x(0, (1,))
        targets(1, 0, 2 * part)
        g_z(1, (3, 2))
        targets(1, 2 * part, 3 * part)
        g_x(0, (3, 2))
        l_col(0, 0)
        g_x(1, (1,))
        targets(1, 3 * part, nblk)
        g_relay(0)
        l_col(0, 1)
        g_x(1, (3, 2))
        l_col(0, 2)
        sq_final()
        l_col(0, 3)
        softmax(0)
        l_col(1, 0)
        g_relay(1)
        l_col(1, 1)
        l_col(1, 2)
        stat_second(0)
        l_col(1, 3)
        softmax(1)
        stat_final(0)
        make_gl(0)
        mm(0, 0)
        mm(0, 1)
        rs_col(0, 0)
        stat_second(1)
        mm(0, 2)
        mm(0, 3)
        rs_col(0, 1)
        rs_col(0, 2)
        stat_final(1)
        make_gl(1)
        loads[4].wait()
        mm(1, 0)
        mm(1, 1)
        rs_col(1, 0)
        dp_send()
        mm(1, 2)
        mm(1, 3)
        rs_col(1, 1)
        rs_col(1, 2)
        rs_col(0, 3)
        dp_final()
        finish(0)
        rs_col(1, 3)
        finish(1)

    outs = [
        pltpu.make_async_copy(a, b, local_sem.at[9 + i])
        for i, (a, b) in enumerate([(lossv, loss_out), (meanv, mean_out), (gradv, grad_out)])
    ]
    for cp in outs:
        cp.start()
    for cp in sends:
        cp.wait_send()
    for cp in outs:
        cp.wait()


NB_TOKENS = 1


def write_out(loss, mean, grad, loss_out, mean_out, grad_out):
    loss_out[...] = loss[...]
    mean_out[...] = mean[0:1, 0:1]
    grad_out[...] = grad[...]


def shards(hidden_rows, norm_gain, head_weight, teacher_ids, teacher_logits, token_weights):
    T, FD = hidden_rows.shape
    VS = head_weight.shape[1]
    K = teacher_ids.shape[1]
    ndp = lax.axis_size("dp")
    NB = NB_TOKENS
    TB = T // NB
    Q = TB // 128
    any_ = pl.BlockSpec(memory_space=pl.ANY)
    V = pltpu.VMEM
    dma = pltpu.SemaphoreType.DMA
    scratch = [
        V((FD, T), F32), V((NZ * NX, 128), F32), V((NZ, NX, NC * FD, VS), BF16),
        V((K, T), jnp.int32), V((K, T), F32), V((T // 128, 128), F32),
        V((128, 128), F32),
        V((NB, NZ, NX, NC, FD, TB), BF16),
        V((TB, NZ * NC * FD), BF16),
        V((NB, TB, VS), F32),
        V((NB, TB, VS), F32),
        V((TB, VS), BF16),
        V((T, 8 * K), F32), V((T, 8 * K), F32), V((T, 8 * K), F32), V((T, 8 * K), F32),
        V((T, 128), F32), V((TB, 128), F32), V((4, TB, 128), F32),
        V((NX * NC, 8, 128), F32), V((NZ, 8, 128), F32),
        V((NB, NX * NC, 4 * Q, 128), F32), V((NB, NZ, 4 * Q, 128), F32),
        V((ndp, 8, 128), F32), V((T // 128, 128), F32), V((3, 8, 128), F32),
        V((NB, 4, NZ, NC, FD, TB), F32),
        V((NB, 4, NZ, FD, TB), BF16), V((NB, 4, NZ, FD, TB), BF16),
        V((NB, 2, NZ, FD // 2, TB), BF16), V((NB, 2, NZ, FD // 2, TB), BF16),
        V((NB, 2, NZ, FD, TB), BF16), V((NB, 2, NZ, FD, TB), BF16),
        V((NB, NZ, FD, TB), BF16), V((NB, NZ, FD, TB), BF16),
        V((T // 128, 128), F32), V((8, 128), F32), V((FD, T), F32),
        dma((12,)), dma((NB, 36)), dma((NB, 35)), dma((12,)), dma((10,)),
        dma((NB, 12)), dma((NB, 10)), dma((ndp,)), dma((ndp,)), dma((NB, 24)), dma((NB, 23)),
    ]
    loss, mean, grad = pl.pallas_call(
        functools.partial(kernel, (NB, TB, VS, ndp, T * ndp)),
        out_shape=(
            jax.ShapeDtypeStruct((T // 128, 128), F32),
            jax.ShapeDtypeStruct((8, 128), F32),
            jax.ShapeDtypeStruct((FD, T), F32),
        ),
        in_specs=[any_] * 6,
        out_specs=(any_, any_, any_),
        scratch_shapes=scratch,
        compiler_params=pltpu.CompilerParams(
            collective_id=0, has_side_effects=True, vmem_limit_bytes=60 * 1024 * 1024
        ),
    )(
        hidden_rows.T,
        norm_gain.reshape(NZ * NX, 128),
        head_weight.reshape(NZ, NX, NC * FD, VS),
        teacher_ids.T,
        teacher_logits.T,
        token_weights.reshape(T // 128, 128),
    )
    loss, mean, grad = pl.pallas_call(
        write_out,
        out_shape=(
            jax.ShapeDtypeStruct((T // 128, 128), F32),
            jax.ShapeDtypeStruct((1, 1), F32),
            jax.ShapeDtypeStruct((FD, T), F32),
        ),
    )(loss, mean, grad)
    return (loss.reshape(T), mean.reshape(()), grad.T)


def solution(mesh):
    in_specs = (P("dp", "segment"), P(), P(None, "segment"), P("dp", None), P("dp", None), P("dp"))
    out_specs = (P("dp"), P(), P("dp", "segment"))
    return jax.shard_map(shards, mesh=mesh, in_specs=in_specs, out_specs=out_specs, check_vma=False)
```
